512 devices in a mesh: attn: 16 (over z, x_hi), exp: 32 (over x_lo, y, core).
Axes of the slice: x: 4 (x_hi: 2, x_lo: 2; x = x_hi * 2 + x_lo), y: 8, z: 8, core: 2. Of those that a mesh axis runs over, the one named last changes fastest.
Arguments:
- residual: bfloat16 [4096, 2880], P(('exp', 'attn')), may hold values from -16 to 16
- queries: bfloat16 [4096, 2048], P(('exp', 'attn')), may hold values from -6 to 6
- window_key_value_cache: bfloat16 [4096, 4, 128, 128], P(('exp', 'attn')), may hold values from -6 to 6
- new_key_value: bfloat16 [4096, 4, 128], P(('exp', 'attn')), may hold values from -5.5 to 5.5
- head_sink_logits: float32 [32], replicated, may hold values from 0 to 5
- out_proj: bfloat16 [2048, 2880], P('attn'), may hold values from -0.125 to 0.125
- norm_gain: float32 [2880], replicated, may hold values from 0.5 to 1.5
- expert_ids: int32 [4096, 4], P('exp'), may hold values from 0 to 31, as said below
- gate_mix: float32 [4096, 4], P('exp'), may hold values from 0.05 to 0.6
- w_gate: bfloat16 [32, 2880, 2880], P('exp', None, 'attn'), may hold values from -0.109375 to 0.109375
- w_up: bfloat16 [32, 2880, 2880], P('exp', None, 'attn'), may hold values from -0.109375 to 0.109375
- w_down: bfloat16 [32, 2880, 2880], P('exp', 'attn'), may hold values from -0.109375 to 0.109375
Outputs:
- layer_out: bfloat16 [4096, 2880], P(('exp', 'attn'))
The draws below stay inside these ranges and needn't reach their ends.
Inputs may be any that keep to these rules, and one draw needn't show every extreme that they name: `expert_ids`: each row names 4 different experts. Within the rows of one index of exp (aligned blocks of 128 rows) no expert is named more than 32 times, and one expert is named exactly 32 times in every block.
All inputs are finite; a program needn't handle non-finite values.
Results may differ from the reference program's by a relative error of at most 0.02.
Values may be sent and summed in bfloat16 or wider, within the bound.
No kernel may reach another device: no remote copies, remote signals or barrier semaphores. Data moves between devices by JAX's collectives and lax.ppermute only.
A program may use at most 128 MiB of HBM per device.

```python
import jax
import jax.numpy as jnp
from jax import lax

D = 2880
FF = 2880
HEAD_SIZE = 64
WINDOW_LENGTH = 128
TOPK = 4
QUERY_HEADS = 32
KEY_VALUE_HEADS = 4
EXPERTS = 32
EXPERT_COLUMN_ROWS = 128
DECODE_ROWS = 4096
CAP = 32
N_ATTN = 16
N_EXP = 32


def draw_queries(key, part):
    key = jax.random.fold_in(key, 1)
    values = jnp.clip(1.5 * jax.random.normal(key, (DECODE_ROWS, QUERY_HEADS * HEAD_SIZE), jnp.float32), -5.5, 5.5)
    return values.astype(jnp.bfloat16)


def draw_window_key_value_cache(key, part):
    key = jax.random.fold_in(key, 2)
    array_shape = (DECODE_ROWS, KEY_VALUE_HEADS, WINDOW_LENGTH, 2 * HEAD_SIZE)
    values = jnp.clip(1.5 * jax.random.normal(key, array_shape, jnp.float32), -5.5, 5.5)
    return values.astype(jnp.bfloat16)


def draw_residual(key, part):
    key = jax.random.fold_in(key, 3)
    values = jnp.clip(jax.random.normal(key, (DECODE_ROWS, D), jnp.float32), -4.0, 4.0)
    return values.astype(jnp.bfloat16)


def draw_expert_ids(key, part):
    key = jax.random.fold_in(key, 4)
    hot_expert = jax.random.randint(jax.random.fold_in(key, 1000), (), 0, EXPERTS)
    assigned = EXPERT_COLUMN_ROWS * TOPK
    spare_count = assigned - CAP

    def one_block(block_key):
        pick_key, order_key = jax.random.split(block_key)
        unit_order = jax.random.permutation(pick_key, (EXPERTS - 1) * CAP)
        others = unit_order[:spare_count] // CAP
        owners = others + (others >= hot_expert).astype(jnp.int32)
        counts = jnp.zeros((EXPERTS,), jnp.int32).at[owners].add(1).at[hot_expert].set(CAP)
        bounds = jnp.cumsum(counts)
        positions = jnp.arange(assigned, dtype=jnp.int32)
        labels = jnp.sum((positions[:, None] >= bounds[None, :]).astype(jnp.int32), axis=1)
        label_table = labels.reshape(TOPK, EXPERT_COLUMN_ROWS).T
        shuffle = jax.random.permutation(order_key, EXPERT_COLUMN_ROWS)
        return label_table[shuffle]

    def block_key_of(index):
        return jax.random.fold_in(key, index)
    block_keys = jax.vmap(block_key_of)(jnp.arange(DECODE_ROWS // EXPERT_COLUMN_ROWS))
    return jax.vmap(one_block)(block_keys).reshape(DECODE_ROWS, TOPK).astype(jnp.int32)


def steps_of(key, extent, cuts, least, high):
    level, own = 1.0, jax.random.fold_in(key, 6)
    for dim, blocks in cuts:
        steps = jnp.exp(jax.random.uniform(jax.random.fold_in(own, dim), (blocks,), jnp.float32, least / len(cuts), high / len(cuts)))
        level = level * jnp.repeat(steps, extent[dim] // blocks).reshape([-1 if axis == dim else 1 for axis in range(len(extent))])
    return level


def centred(key, shape, width, reach, shards=(), kind=jnp.bfloat16):
    values = jax.random.normal(key, shape, jnp.float32) * width
    if len(shards) > 0:
        values = steps_of(key, shape, shards, -0.22, 0.18) * values
    return jnp.clip(values, min=-reach, max=reach).astype(kind)


def setup_inputs(seed: int = 0) -> dict:
    arg_keys = jax.random.split(jax.random.key(seed), 13)
    residual = draw_residual(jax.random.fold_in(arg_keys[12], 71), 0)
    queries = draw_queries(jax.random.fold_in(arg_keys[12], 71), 0)
    window_key_value_cache = draw_window_key_value_cache(jax.random.fold_in(arg_keys[12], 71), 0)
    new_key_value = centred(arg_keys[3], (DECODE_ROWS, KEY_VALUE_HEADS, 2 * HEAD_SIZE), 1.5, 5.5, ((0, 512),))
    head_sink_logits = jnp.clip(jax.random.uniform(arg_keys[4], (QUERY_HEADS,), jnp.float32, 0.0, 5.0), 0.0, 5.0)
    out_proj = centred(arg_keys[5], (QUERY_HEADS * HEAD_SIZE, D), (QUERY_HEADS * HEAD_SIZE) ** -0.5, 0.125, ((0, 16),))
    norm_gain = jnp.clip(1.0 + 0.1 * jax.random.normal(arg_keys[6], (D,), jnp.float32), 0.5, 1.5)
    expert_ids = draw_expert_ids(jax.random.fold_in(arg_keys[12], 71), 0)
    gate_mix = jnp.clip(0.05 + 0.55 * jax.random.uniform(arg_keys[8], (DECODE_ROWS, TOPK), jnp.float32) ** steps_of(arg_keys[8], (DECODE_ROWS, TOPK), ((0, 32),), -0.2, 0.2), 0.05, 0.6)
    w_gate = centred(arg_keys[9], (EXPERTS, D, FF), D ** -0.5, 0.109375, ((0, 32), (2, 16)))
    w_up = centred(arg_keys[10], (EXPERTS, D, FF), D ** -0.5, 0.109375, ((0, 32), (2, 16)))
    w_down = centred(arg_keys[11], (EXPERTS, FF, D), FF ** -0.5, 0.109375, ((0, 32), (1, 16)))
    return dict(residual=residual, queries=queries, window_key_value_cache=window_key_value_cache, new_key_value=new_key_value, head_sink_logits=head_sink_logits, out_proj=out_proj, norm_gain=norm_gain, expert_ids=expert_ids, gate_mix=gate_mix, w_gate=w_gate, w_up=w_up, w_down=w_down)


def attend(queries, window_key_value_cache, new_key_value, head_sink_logits):
    count_of_rows = queries.shape[0]
    query_groups = QUERY_HEADS // KEY_VALUE_HEADS
    grouped_queries = queries.astype(jnp.float32).reshape(count_of_rows, KEY_VALUE_HEADS, query_groups, HEAD_SIZE)
    all_keys = jnp.concatenate([window_key_value_cache[:, :, :, :HEAD_SIZE], new_key_value[:, :, None, :HEAD_SIZE]], axis=2).astype(jnp.float32)
    all_values = jnp.concatenate([window_key_value_cache[:, :, :, HEAD_SIZE:], new_key_value[:, :, None, HEAD_SIZE:]], axis=2).astype(jnp.float32)
    scores = jnp.einsum('rkgd,rkjd->rkgj', grouped_queries, all_keys) * HEAD_SIZE ** (-0.5)
    sink_portion = head_sink_logits.reshape(1, KEY_VALUE_HEADS, query_groups, 1)
    highest = jnp.maximum(lax.optimization_barrier(jnp.max(scores, axis=3, keepdims=True)), sink_portion)
    raised = jnp.exp(scores - highest)
    denominator = lax.optimization_barrier(jnp.sum(raised, axis=3, keepdims=True)) + jnp.exp(sink_portion - highest)
    weights = lax.optimization_barrier((raised / denominator).astype(jnp.bfloat16)).astype(jnp.float32)
    combined = jnp.einsum('rkgj,rkjd->rkgd', weights, all_values)
    return combined.reshape(count_of_rows, QUERY_HEADS * HEAD_SIZE).astype(jnp.bfloat16)

def window_attend_block(parts):
    return attend(parts[0], parts[1], parts[2], parts[3])

def reference(residual, queries, window_key_value_cache, new_key_value, head_sink_logits, out_proj, norm_gain, expert_ids, gate_mix, w_gate, w_up, w_down):
    sink_logit_copies = jnp.broadcast_to(head_sink_logits[None, :], (N_EXP, QUERY_HEADS))
    attention_output = lax.map(window_attend_block, (queries.reshape(N_EXP, EXPERT_COLUMN_ROWS, QUERY_HEADS * HEAD_SIZE), window_key_value_cache.reshape(N_EXP, EXPERT_COLUMN_ROWS, KEY_VALUE_HEADS, WINDOW_LENGTH, 2 * HEAD_SIZE), new_key_value.reshape(N_EXP, EXPERT_COLUMN_ROWS, KEY_VALUE_HEADS, 2 * HEAD_SIZE), sink_logit_copies))
    attention_output = attention_output.reshape(DECODE_ROWS, QUERY_HEADS * HEAD_SIZE)
    hidden_state = residual.astype(jnp.float32) + jnp.dot(attention_output, out_proj, preferred_element_type=jnp.float32)
    mean_square = lax.optimization_barrier(jnp.mean(hidden_state * hidden_state, axis=1, keepdims=True))
    normed = (hidden_state * lax.rsqrt(mean_square + 1e-05) * norm_gain).astype(jnp.bfloat16)
    flat_ids = expert_ids.reshape(N_EXP, EXPERT_COLUMN_ROWS * TOPK)
    onehot_table = (flat_ids[:, :, None] == jnp.arange(EXPERTS, dtype=jnp.int32)[None, None, :]).astype(jnp.int32)
    slot_index = lax.optimization_barrier(jnp.sum((jnp.cumsum(onehot_table, axis=1) - 1) * onehot_table, axis=2))
    column_index = jnp.arange(N_EXP, dtype=jnp.int32)[:, None]
    places = (flat_ids * N_EXP + column_index) * CAP + slot_index
    row_number = column_index * EXPERT_COLUMN_ROWS + jnp.arange(EXPERT_COLUMN_ROWS * TOPK, dtype=jnp.int32)[None, :] // TOPK
    row_table = jnp.full((EXPERTS * N_EXP * CAP,), DECODE_ROWS, jnp.int32).at[places.reshape(-1)].set(row_number.reshape(-1).astype(jnp.int32))
    row_table = row_table.reshape(EXPERTS, N_EXP * CAP)
    gate_table = jnp.zeros((EXPERTS * N_EXP * CAP,), jnp.float32).at[places.reshape(-1)].set(gate_mix.reshape(-1))
    gate_table = gate_table.reshape(EXPERTS, N_EXP * CAP)
    padded = jnp.concatenate([normed, jnp.zeros((1, D), jnp.bfloat16)], axis=0)
    slice_width = FF // N_ATTN

    def one_expert(carry, parts):
        rows_used, gates_used, gate_weight, up_weight, down_weight = parts
        inputs = jnp.take(padded, rows_used, axis=0)
        gate_proj = jnp.dot(inputs, gate_weight, preferred_element_type=jnp.float32)
        up_proj = jnp.dot(inputs, up_weight, preferred_element_type=jnp.float32)
        activated = (gate_proj * jax.nn.sigmoid(1.702 * gate_proj) * (up_proj + 1.0)).astype(jnp.bfloat16)
        pieces = jnp.einsum('naf,afd->nad', activated.astype(jnp.float32).reshape(N_EXP * CAP, N_ATTN, slice_width), down_weight.astype(jnp.float32).reshape(N_ATTN, slice_width, D))
        rounded = lax.optimization_barrier(pieces.astype(jnp.bfloat16)).astype(jnp.float32)
        summed = lax.optimization_barrier(jnp.sum(rounded, axis=1))
        carry = carry.at[rows_used].add(gates_used[:, None] * summed)
        return (carry, rows_used)
    start_value = jnp.zeros((DECODE_ROWS + 1, D), jnp.float32)
    mixed = lax.scan(one_expert, start_value, (row_table, gate_table, w_gate, w_up, w_down))[0]
    return (hidden_state + mixed[:DECODE_ROWS]).astype(jnp.bfloat16)
```

```python
import jax
import jax.numpy as jnp
from jax import lax
from jax.experimental import pallas as pl
from jax.experimental.pallas import tpu as pltpu
from jax.sharding import PartitionSpec as P

HEAD_SIZE = 64
QUERY_HEADS = 32
KEY_VALUE_HEADS = 4
D = 2880
FF_LOCAL = 180
N_ATTN = 16
N_EXP = 32
CAP = 32
HALVES = 2
BLOCKS = N_ATTN // HALVES
BLOCK = D // BLOCKS
LANES = 384
FF_LANES = 256
ROW_TILE = 256
F32 = jnp.float32
BF16 = jnp.bfloat16

Z_GROUPS = [[z * HALVES + half for z in range(BLOCKS)] for half in range(HALVES)]


def attend(queries, window_key_value_cache, new_key_value, head_sink_logits):
    count_of_rows = queries.shape[0]
    query_groups = QUERY_HEADS // KEY_VALUE_HEADS
    grouped_queries = queries.reshape(count_of_rows, KEY_VALUE_HEADS, query_groups, HEAD_SIZE)
    all_keys = jnp.concatenate(
        [window_key_value_cache[:, :, :, :HEAD_SIZE], new_key_value[:, :, None, :HEAD_SIZE]], axis=2
    )
    all_values = jnp.concatenate(
        [window_key_value_cache[:, :, :, HEAD_SIZE:], new_key_value[:, :, None, HEAD_SIZE:]], axis=2
    )
    scores = jnp.einsum(
        "rkgd,rkjd->rkgj", grouped_queries, all_keys, preferred_element_type=jnp.float32
    ) * HEAD_SIZE ** (-0.5)
    sink_portion = head_sink_logits.reshape(1, KEY_VALUE_HEADS, query_groups, 1)
    highest = jnp.maximum(jnp.max(scores, axis=3, keepdims=True), sink_portion)
    raised = jnp.exp(scores - highest)
    denominator = jnp.sum(raised, axis=3, keepdims=True) + jnp.exp(sink_portion - highest)
    weights = (raised / denominator).astype(jnp.bfloat16)
    combined = jnp.einsum(
        "rkgj,rkjd->rkgd", weights, all_values, preferred_element_type=jnp.float32
    )
    return combined.reshape(count_of_rows, QUERY_HEADS * HEAD_SIZE).astype(jnp.bfloat16)


def experts_kernel(x_ref, w_in_ref, w_out_ref, y_ref):
    square = jnp.zeros((ROW_TILE, 1), F32)
    both = jnp.zeros((ROW_TILE, 2 * FF_LANES), F32)
    for block in range(BLOCKS):
        x = x_ref[block]
        parts = x[:, LANES - 128 :].astype(F32)
        at = BLOCK - (LANES - 128)
        square = square + parts[:, at : at + 1] + parts[:, at + 1 : at + 2]
        both = both + jnp.dot(x, w_in_ref[block], preferred_element_type=F32)
    both = both * lax.rsqrt(square * (1.0 / D) + 1e-05)
    gate = both[:, :FF_LANES]
    up = both[:, FF_LANES:]
    hidden = (gate * jax.nn.sigmoid(1.702 * gate) * (up + 1.0)).astype(BF16)
    for block in range(BLOCKS):
        y_ref[block] = jnp.dot(hidden, w_out_ref[block], preferred_element_type=F32).astype(BF16)


def run_experts(x, w_in, w_out):
    rows = x.shape[1]
    return pl.pallas_call(
        experts_kernel,
        grid=(rows // ROW_TILE,),
        in_specs=[
            pl.BlockSpec((BLOCKS, ROW_TILE, LANES), lambda i: (0, i, 0)),
            pl.BlockSpec((BLOCKS, LANES, 2 * FF_LANES), lambda i: (0, 0, 0)),
            pl.BlockSpec((BLOCKS, FF_LANES, LANES), lambda i: (0, 0, 0)),
        ],
        out_specs=pl.BlockSpec((BLOCKS, ROW_TILE, LANES), lambda i: (0, i, 0)),
        out_shape=jax.ShapeDtypeStruct((BLOCKS, rows, LANES), BF16),
        compiler_params=pltpu.CompilerParams(vmem_limit_bytes=40 * 2**20),
        cost_estimate=pl.CostEstimate(
            flops=2 * rows * D * 3 * FF_LOCAL, bytes_accessed=18 * 2**20, transcendentals=rows * FF_LOCAL
        ),
    )(x, w_in, w_out)


def to_blocks(array):
    array = array.reshape(array.shape[:-1] + (BLOCKS, BLOCK))
    return jnp.pad(array, [(0, 0)] * (array.ndim - 1) + [(0, LANES - BLOCK)])


def local(
    residual,
    queries,
    window_key_value_cache,
    new_key_value,
    head_sink_logits,
    out_proj,
    norm_gain,
    expert_ids,
    gate_mix,
    w_gate,
    w_up,
    w_down,
):
    own_rows = residual.shape[0]
    column_rows = expert_ids.shape[0]
    attn_index = lax.axis_index("attn")
    z_index = attn_index // HALVES

    other_proj = lax.ppermute(out_proj, "attn", [(i, i ^ 1) for i in range(N_ATTN)])

    attended = attend(queries, window_key_value_cache, new_key_value, head_sink_logits)
    heads = attended.reshape(own_rows, BLOCKS, HALVES, 128).transpose(1, 2, 0, 3)
    residual_blocks = to_blocks(residual).transpose(1, 0, 2)
    residual_blocks = jnp.broadcast_to(residual_blocks[:, None], (BLOCKS, HALVES, own_rows, LANES))
    sent = jnp.concatenate([heads, heads[:, ::-1], residual_blocks], axis=3)
    got = lax.all_to_all(sent.reshape(N_ATTN, own_rows, 256 + LANES), "attn", 0, 0, tiled=True)
    got = got.reshape(column_rows, 256 + LANES)

    proj = to_blocks(jnp.concatenate([out_proj, other_proj], axis=0)).transpose(1, 0, 2)
    partial_sums = jnp.einsum("rk,zkd->zrd", got[:, :256], proj, preferred_element_type=F32).astype(BF16)
    sums = lax.all_to_all(partial_sums, "attn", 0, 0, tiled=True, axis_index_groups=Z_GROUPS)
    hidden_state = got[:, 256:].astype(F32) + jnp.sum(sums.astype(F32), axis=0)

    gain = lax.dynamic_index_in_dim(to_blocks(norm_gain), z_index, 0, keepdims=False)
    square = jnp.sum(hidden_state * hidden_state, axis=1, keepdims=True)
    square_high = lax.reduce_precision(square, 8, 7)
    square_low = square - square_high
    lane = lax.broadcasted_iota(jnp.int32, (column_rows, LANES), 1)
    scaled = hidden_state * gain
    scaled = jnp.where(lane == BLOCK, square_high, jnp.where(lane == BLOCK + 1, square_low, scaled)).astype(BF16)

    names = expert_ids.T[None, :, :] == jnp.arange(N_EXP, dtype=jnp.int32)[:, None, None]
    named = jnp.any(names, axis=1)
    weight = jnp.sum(jnp.where(names, gate_mix.T[None, :, :], 0.0), axis=1)
    row = jnp.arange(column_rows, dtype=jnp.int32)
    earlier = (row[:, None] < row[None, :]).astype(BF16)
    slot = jnp.dot(named.astype(BF16), earlier, preferred_element_type=F32).astype(jnp.int32)
    slot = jnp.where(named, slot, -1)
    taken = slot[:, None, :] == jnp.arange(CAP, dtype=jnp.int32)[None, :, None]
    select = taken.astype(BF16).reshape(N_EXP * CAP, column_rows)
    mix = jnp.where(taken, weight[:, None, :], 0.0).reshape(N_EXP * CAP, column_rows)
    mix_high = lax.reduce_precision(mix, 8, 7)
    mix_low = (mix - mix_high).astype(BF16)
    mix_high = mix_high.astype(BF16)

    outgoing = jnp.dot(select, scaled, preferred_element_type=F32).astype(BF16)
    outgoing = outgoing.reshape(N_EXP, CAP, LANES)
    incoming = lax.all_to_all(outgoing, "exp", 0, 0, tiled=True).reshape(N_EXP * CAP, LANES)
    rows_in = lax.all_gather(incoming, "attn", axis=0, tiled=True, axis_index_groups=Z_GROUPS)

    def padded_in(w):
        w = w.reshape(BLOCKS, BLOCK, FF_LOCAL)
        return jnp.pad(w, ((0, 0), (0, LANES - BLOCK), (0, FF_LANES - FF_LOCAL)))

    w_in = jnp.concatenate([padded_in(w_gate), padded_in(w_up)], axis=2)
    w_out = jnp.pad(to_blocks(w_down[0]).transpose(1, 0, 2), ((0, 0), (0, FF_LANES - FF_LOCAL), (0, 0)))
    rows_out = run_experts(rows_in.reshape(BLOCKS, N_EXP * CAP, LANES), w_in, w_out)

    summed = lax.psum_scatter(
        rows_out.reshape(BLOCKS * N_EXP * CAP, LANES),
        "attn",
        scatter_dimension=0,
        tiled=True,
        axis_index_groups=Z_GROUPS,
    )
    returned = lax.all_to_all(summed.reshape(N_EXP, CAP, LANES), "exp", 0, 0, tiled=True)
    returned = returned.reshape(N_EXP * CAP, LANES)
    over_slots = (((0,), (0,)), ((), ()))
    mixed = lax.dot_general(mix_high, returned, over_slots, preferred_element_type=F32)
    mixed = mixed + lax.dot_general(mix_low, returned, over_slots, preferred_element_type=F32)
    first_half = attn_index % HALVES == 0
    mixed = mixed + jnp.where(first_half, hidden_state, 0.0)

    last = lax.all_to_all(mixed.reshape(N_ATTN, own_rows, LANES), "attn", 0, 0, tiled=True)
    last = jnp.sum(last.reshape(BLOCKS, HALVES, own_rows, LANES), axis=1)
    return last[:, :, :BLOCK].transpose(1, 0, 2).reshape(own_rows, D).astype(BF16)


def solution(mesh):
    in_specs = (
        P(("exp", "attn"), None),
        P(("exp", "attn"), None),
        P(("exp", "attn"), None, None, None),
        P(("exp", "attn"), None, None),
        P(),
        P("attn", None),
        P(),
        P("exp", None),
        P("exp", None),
        P("exp", None, "attn"),
        P("exp", None, "attn"),
        P("exp", "attn", None),
    )
    out_specs = P(("exp", "attn"), None)
    return jax.shard_map(local, mesh=mesh, in_specs=in_specs, out_specs=out_specs, check_vma=False)
```

```python
import jax
import jax.numpy as jnp
from jax import lax
from jax.sharding import PartitionSpec as P

HEAD_SIZE = 64
QUERY_HEADS = 32
KEY_VALUE_HEADS = 4
D = 2880
FF_LOCAL = 180
N_ATTN = 16
N_EXP = 32
CAP = 32
HALVES = 2
BLOCKS = N_ATTN // HALVES
BLOCK = D // BLOCKS
LANES = 384
FF_LANES = 256
FAR = BLOCKS // 2
F32 = jnp.float32
BF16 = jnp.bfloat16

Z_GROUPS = [[z * HALVES + half for z in range(BLOCKS)] for half in range(HALVES)]


def attend(queries, window_key_value_cache, new_key_value, head_sink_logits):
    count_of_rows = queries.shape[0]
    query_groups = QUERY_HEADS // KEY_VALUE_HEADS
    grouped_queries = queries.reshape(count_of_rows, KEY_VALUE_HEADS, query_groups, HEAD_SIZE)
    all_keys = jnp.concatenate(
        [window_key_value_cache[:, :, :, :HEAD_SIZE], new_key_value[:, :, None, :HEAD_SIZE]], axis=2
    )
    all_values = jnp.concatenate(
        [window_key_value_cache[:, :, :, HEAD_SIZE:], new_key_value[:, :, None, HEAD_SIZE:]], axis=2
    )
    scores = jnp.einsum(
        "rkgd,rkjd->rkgj", grouped_queries, all_keys, preferred_element_type=jnp.float32
    ) * HEAD_SIZE ** (-0.5)
    sink_portion = head_sink_logits.reshape(1, KEY_VALUE_HEADS, query_groups, 1)
    highest = jnp.maximum(jnp.max(scores, axis=3, keepdims=True), sink_portion)
    raised = jnp.exp(scores - highest)
    denominator = jnp.sum(raised, axis=3, keepdims=True) + jnp.exp(sink_portion - highest)
    weights = (raised / denominator).astype(jnp.bfloat16)
    combined = jnp.einsum(
        "rkgj,rkjd->rkgd", weights, all_values, preferred_element_type=jnp.float32
    )
    return combined.reshape(count_of_rows, QUERY_HEADS * HEAD_SIZE).astype(jnp.bfloat16)


def shift_over_z(array, step):
    pairs = [
        (z * HALVES + half, (z + step) % BLOCKS * HALVES + half) for z in range(BLOCKS) for half in range(HALVES)
    ]
    return lax.ppermute(array, "attn", pairs)


def to_blocks(array):
    array = array.reshape(array.shape[:-1] + (BLOCKS, BLOCK))
    return jnp.pad(array, [(0, 0)] * (array.ndim - 1) + [(0, LANES - BLOCK)])


def local(
    residual,
    queries,
    window_key_value_cache,
    new_key_value,
    head_sink_logits,
    out_proj,
    norm_gain,
    expert_ids,
    gate_mix,
    w_gate,
    w_up,
    w_down,
):
    own_rows = residual.shape[0]
    column_rows = expert_ids.shape[0]
    attn_index = lax.axis_index("attn")
    z_index = attn_index // HALVES

    other_proj = lax.ppermute(out_proj, "attn", [(i, i ^ 1) for i in range(N_ATTN)])

    attended = attend(queries, window_key_value_cache, new_key_value, head_sink_logits)
    heads = attended.reshape(own_rows, BLOCKS, HALVES, 128).transpose(1, 2, 0, 3)
    residual_blocks = to_blocks(residual).transpose(1, 0, 2)
    residual_blocks = jnp.broadcast_to(residual_blocks[:, None], (BLOCKS, HALVES, own_rows, LANES))
    sent = jnp.concatenate([heads, heads[:, ::-1], residual_blocks], axis=3)
    got = lax.all_to_all(sent.reshape(N_ATTN, own_rows, 256 + LANES), "attn", 0, 0, tiled=True)
    got = got.reshape(column_rows, 256 + LANES)

    proj = to_blocks(jnp.concatenate([out_proj, other_proj], axis=0)).transpose(1, 0, 2)
    partial_sums = jnp.einsum("rk,zkd->zrd", got[:, :256], proj, preferred_element_type=F32).astype(BF16)
    sums = lax.all_to_all(partial_sums, "attn", 0, 0, tiled=True, axis_index_groups=Z_GROUPS)
    hidden_state = got[:, 256:].astype(F32) + jnp.sum(sums.astype(F32), axis=0)

    gain = lax.dynamic_index_in_dim(to_blocks(norm_gain), z_index, 0, keepdims=False)
    square = jnp.sum(hidden_state * hidden_state, axis=1, keepdims=True)
    square_high = lax.reduce_precision(square, 8, 7)
    square_low = square - square_high
    lane = lax.broadcasted_iota(jnp.int32, (column_rows, LANES), 1)
    scaled = hidden_state * gain
    scaled = jnp.where(lane == BLOCK, square_high, jnp.where(lane == BLOCK + 1, square_low, scaled)).astype(BF16)

    names = expert_ids.T[None, :, :] == jnp.arange(N_EXP, dtype=jnp.int32)[:, None, None]
    named = jnp.any(names, axis=1)
    weight = jnp.sum(jnp.where(names, gate_mix.T[None, :, :], 0.0), axis=1)
    row = jnp.arange(column_rows, dtype=jnp.int32)
    earlier = (row[:, None] < row[None, :]).astype(BF16)
    slot = jnp.dot(named.astype(BF16), earlier, preferred_element_type=F32).astype(jnp.int32)
    slot = jnp.where(named, slot, -1)
    taken = slot[:, None, :] == jnp.arange(CAP, dtype=jnp.int32)[None, :, None]
    select = taken.astype(BF16).reshape(N_EXP * CAP, column_rows)
    mix = jnp.where(taken, weight[:, None, :], 0.0).reshape(N_EXP * CAP, column_rows)
    mix_high = lax.reduce_precision(mix, 8, 7)
    mix_low = (mix - mix_high).astype(BF16)
    mix_high = mix_high.astype(BF16)

    def dispatch(rows):
        outgoing = jnp.dot(select, rows, preferred_element_type=F32).astype(BF16)
        incoming = lax.all_to_all(outgoing.reshape(N_EXP, CAP, LANES), "exp", 0, 0, tiled=True)
        return incoming.reshape(N_EXP * CAP, LANES)

    def collect(partial_value):
        returned = lax.all_to_all(partial_value.reshape(N_EXP, CAP, LANES), "exp", 0, 0, tiled=True)
        returned = returned.reshape(N_EXP * CAP, LANES)
        over_slots = (((0,), (0,)), ((), ()))
        mixed = lax.dot_general(mix_high, returned, over_slots, preferred_element_type=F32)
        return mixed + lax.dot_general(mix_low, returned, over_slots, preferred_element_type=F32)

    def padded_in(w):
        w = w.reshape(BLOCKS, BLOCK, FF_LOCAL)
        return jnp.pad(w, ((0, 0), (0, LANES - BLOCK), (0, FF_LANES - FF_LOCAL)))

    def own_first(blocks):
        return lax.dynamic_slice_in_dim(jnp.concatenate([blocks, blocks]), z_index, BLOCKS, 0)

    w_in = jnp.concatenate([padded_in(w_gate), padded_in(w_up)], axis=2)
    in_row = lax.broadcasted_iota(jnp.int32, w_in.shape, 1)
    in_column = lax.broadcasted_iota(jnp.int32, w_in.shape, 2)
    w_in = jnp.where((in_column == FF_LOCAL) & (in_row >= BLOCK) & (in_row < BLOCK + 2), jnp.ones((), BF16), w_in)
    w_in = own_first(w_in)
    w_out = jnp.pad(to_blocks(w_down[0]).transpose(1, 0, 2), ((0, 0), (0, FF_LANES - FF_LOCAL), (0, 0)))
    w_out = own_first(w_out)

    own = dispatch(scaled)
    far = dispatch(shift_over_z(scaled, FAR))
    both = jnp.dot(own, w_in[0], preferred_element_type=F32)
    up_block, down_block = own, own
    for step in range(1, FAR):
        up_block, down_block = shift_over_z(up_block, 1), shift_over_z(down_block, -1)
        both = both + jnp.dot(up_block, w_in[BLOCKS - step], preferred_element_type=F32)
        both = both + jnp.dot(down_block, w_in[step], preferred_element_type=F32)
        if step == FAR - 2:
            both = lax.optimization_barrier(both + jnp.dot(far, w_in[FAR], preferred_element_type=F32))
    both = both * lax.rsqrt(both[:, FF_LOCAL : FF_LOCAL + 1] * (1.0 / D) + 1e-05)
    gate = both[:, :FF_LANES]
    up = both[:, FF_LANES:]
    expert_hidden = (gate * jax.nn.sigmoid(1.702 * gate) * (up + 1.0)).astype(BF16)

    def output_block(offset):
        return jnp.dot(expert_hidden, w_out[offset % BLOCKS], preferred_element_type=F32)

    up_sum = shift_over_z(output_block(FAR - 1).astype(BF16), 1)
    down_sum = shift_over_z(output_block(1 - FAR).astype(BF16), -1)
    far_sum = collect(output_block(FAR).astype(BF16))
    for offset in range(FAR - 2, 0, -1):
        up_sum = shift_over_z((output_block(offset) + up_sum.astype(F32)).astype(BF16), 1)
        down_sum = shift_over_z((output_block(-offset) + down_sum.astype(F32)).astype(BF16), -1)
    own_sum = (output_block(0) + up_sum.astype(F32) + down_sum.astype(F32)).astype(BF16)
    mixed = collect(own_sum) + shift_over_z(far_sum, FAR)
    first_half = attn_index % HALVES == 0
    mixed = mixed + jnp.where(first_half, hidden_state, 0.0)

    last = lax.all_to_all(mixed.reshape(N_ATTN, own_rows, LANES), "attn", 0, 0, tiled=True)
    last = jnp.sum(last.reshape(BLOCKS, HALVES, own_rows, LANES), axis=1)
    return last[:, :, :BLOCK].transpose(1, 0, 2).reshape(own_rows, D).astype(BF16)


def solution(mesh):
    in_specs = (
        P(("exp", "attn"), None),
        P(("exp", "attn"), None),
        P(("exp", "attn"), None, None, None),
        P(("exp", "attn"), None, None),
        P(),
        P("attn", None),
        P(),
        P("exp", None),
        P("exp", None),
        P("exp", None, "attn"),
        P("exp", None, "attn"),
        P("exp", "attn", None),
    )
    out_specs = P(("exp", "attn"), None)
    return jax.shard_map(local, mesh=mesh, in_specs=in_specs, out_specs=out_specs, check_vma=False)
```

```python
import jax
import jax.numpy as jnp
from jax import lax
from jax.sharding import PartitionSpec as P

HEAD_SIZE = 64
QUERY_HEADS = 32
KEY_VALUE_HEADS = 4
D = 2880
FF_LOCAL = 180
N_ATTN = 16
N_EXP = 32
CAP = 32
HALVES = 2
BLOCKS = N_ATTN // HALVES
BLOCK = D // BLOCKS
LANES = 384
FF_LANES = 256
FAR = BLOCKS // 2
F32 = jnp.float32
BF16 = jnp.bfloat16

Z_GROUPS = [[z * HALVES + half for z in range(BLOCKS)] for half in range(HALVES)]


def attend(queries, window_key_value_cache, new_key_value, head_sink_logits):
    count_of_rows = queries.shape[0]
    query_groups = QUERY_HEADS // KEY_VALUE_HEADS
    grouped_queries = queries.reshape(count_of_rows, KEY_VALUE_HEADS, query_groups, HEAD_SIZE)
    all_keys = jnp.concatenate(
        [window_key_value_cache[:, :, :, :HEAD_SIZE], new_key_value[:, :, None, :HEAD_SIZE]], axis=2
    )
    all_values = jnp.concatenate(
        [window_key_value_cache[:, :, :, HEAD_SIZE:], new_key_value[:, :, None, HEAD_SIZE:]], axis=2
    )
    scores = jnp.einsum(
        "rkgd,rkjd->rkgj", grouped_queries, all_keys, preferred_element_type=jnp.float32
    ) * HEAD_SIZE ** (-0.5)
    sink_portion = head_sink_logits.reshape(1, KEY_VALUE_HEADS, query_groups, 1)
    highest = jnp.maximum(jnp.max(scores, axis=3, keepdims=True), sink_portion)
    raised = jnp.exp(scores - highest)
    denominator = jnp.sum(raised, axis=3, keepdims=True) + jnp.exp(sink_portion - highest)
    weights = (raised / denominator).astype(jnp.bfloat16)
    combined = jnp.einsum(
        "rkgj,rkjd->rkgd", weights, all_values, preferred_element_type=jnp.float32
    )
    return combined.reshape(count_of_rows, QUERY_HEADS * HEAD_SIZE).astype(jnp.bfloat16)


def shift_over_z(array, step):
    pairs = [
        (z * HALVES + half, (z + step) % BLOCKS * HALVES + half) for z in range(BLOCKS) for half in range(HALVES)
    ]
    return lax.ppermute(array, "attn", pairs)


def swap_halves(array):
    return lax.ppermute(array, "attn", [(i, i ^ 1) for i in range(N_ATTN)])


def over_z(array):
    return lax.all_to_all(array, "attn", 0, 0, tiled=True, axis_index_groups=Z_GROUPS)


def over_experts(array):
    return lax.all_to_all(array, "exp", 0, 0, tiled=True)


def to_blocks(array):
    array = array.reshape(array.shape[:-1] + (BLOCKS, BLOCK))
    return jnp.pad(array, [(0, 0)] * (array.ndim - 1) + [(0, LANES - BLOCK)])


def local(
    residual,
    queries,
    window_key_value_cache,
    new_key_value,
    head_sink_logits,
    out_proj,
    norm_gain,
    expert_ids,
    gate_mix,
    w_gate,
    w_up,
    w_down,
):
    own_rows = residual.shape[0]
    column_rows = expert_ids.shape[0]
    half_rows = column_rows // HALVES
    half_cap = CAP // HALVES
    half_slots = N_EXP * half_cap
    attn_index = lax.axis_index("attn")
    z_index = lax.shift_right_logical(attn_index, 1)
    half = lax.bitwise_and(attn_index, 1)
    first_half = half == 0

    other_proj = swap_halves(out_proj)
    proj = jnp.concatenate(
        [jnp.where(first_half, out_proj, other_proj), jnp.where(first_half, other_proj, out_proj)], axis=0
    )
    proj = to_blocks(proj).transpose(1, 0, 2)

    attended = attend(queries, window_key_value_cache, new_key_value, head_sink_logits)
    heads = attended.reshape(own_rows, BLOCKS, HALVES * 128)
    sent = jnp.concatenate([heads, to_blocks(residual)], axis=2).transpose(1, 0, 2)
    got = over_z(sent).reshape(half_rows, HALVES * 128 + LANES)
    partial_sums = jnp.einsum("rk,zkd->zrd", got[:, : HALVES * 128], proj, preferred_element_type=F32).astype(BF16)
    hidden_state = got[:, HALVES * 128 :].astype(F32) + jnp.sum(over_z(partial_sums).astype(F32), axis=0)

    gain = lax.dynamic_index_in_dim(to_blocks(norm_gain), z_index, 0, keepdims=False)
    square = jnp.sum(hidden_state * hidden_state, axis=1, keepdims=True)
    square_high = lax.reduce_precision(square, 8, 7)
    square_low = square - square_high
    lane = lax.broadcasted_iota(jnp.int32, (half_rows, LANES), 1)
    scaled = hidden_state * gain
    scaled = jnp.where(lane == BLOCK, square_high, jnp.where(lane == BLOCK + 1, square_low, scaled)).astype(BF16)
    other_scaled = swap_halves(scaled).reshape(BLOCKS, own_rows, LANES)
    scaled = scaled.reshape(BLOCKS, own_rows, LANES)
    scaled = jnp.stack(
        [jnp.where(first_half, scaled, other_scaled), jnp.where(first_half, other_scaled, scaled)], axis=1
    ).reshape(column_rows, LANES)

    names = expert_ids.T[None, :, :] == jnp.arange(N_EXP, dtype=jnp.int32)[:, None, None]
    named = jnp.any(names, axis=1)
    weight = jnp.sum(jnp.where(names, gate_mix.T[None, :, :], 0.0), axis=1)
    row = jnp.arange(column_rows, dtype=jnp.int32)
    earlier = (row[:, None] < row[None, :]).astype(BF16)
    slot = jnp.dot(named.astype(BF16), earlier, preferred_element_type=F32).astype(jnp.int32)
    slot = jnp.where(named, slot, -1)

    def taken_of(own_half):
        base = half_cap * (half if own_half else 1 - half)
        return slot[:, None, :] == base + jnp.arange(half_cap, dtype=jnp.int32)[None, :, None]

    taken_own, taken_other = taken_of(True), taken_of(False)
    taken_both = jnp.concatenate([taken_own, taken_other], axis=1)

    def picked(taken, rows):
        select = taken.astype(BF16).reshape(-1, column_rows)
        return jnp.dot(select, rows, preferred_element_type=F32).astype(BF16).reshape(N_EXP, -1, LANES)

    def mixed_of(taken, partial_value):
        returned = over_experts(partial_value).reshape(-1, LANES)
        mix = jnp.where(taken, weight[:, None, :], 0.0).reshape(-1, column_rows)
        mix_high = lax.reduce_precision(mix, 8, 7)
        mix_low = (mix - mix_high).astype(BF16)
        over_slots = (((0,), (0,)), ((), ()))
        mixed = lax.dot_general(mix_high.astype(BF16), returned, over_slots, preferred_element_type=F32)
        return mixed + lax.dot_general(mix_low, returned, over_slots, preferred_element_type=F32)

    def padded_in(w):
        w = w.reshape(BLOCKS, BLOCK, FF_LOCAL)
        return jnp.pad(w, ((0, 0), (0, LANES - BLOCK), (0, FF_LANES - FF_LOCAL)))

    def own_first(blocks):
        return lax.dynamic_slice_in_dim(jnp.concatenate([blocks, blocks]), z_index, BLOCKS, 0)

    w_in = jnp.concatenate([padded_in(w_gate), padded_in(w_up)], axis=2)
    in_row = lax.broadcasted_iota(jnp.int32, w_in.shape, 1)
    in_column = lax.broadcasted_iota(jnp.int32, w_in.shape, 2)
    w_in = jnp.where((in_column == FF_LOCAL) & (in_row >= BLOCK) & (in_row < BLOCK + 2), jnp.ones((), BF16), w_in)
    w_in = own_first(w_in)
    w_out = jnp.pad(to_blocks(w_down[0]).transpose(1, 0, 2), ((0, 0), (0, FF_LANES - FF_LOCAL), (0, 0)))
    w_out = own_first(w_out)

    far_outgoing = picked(taken_both, shift_over_z(scaled, FAR))
    own = over_experts(picked(taken_own, scaled)).reshape(half_slots, LANES)
    own, w_in, w_out, far_outgoing = lax.optimization_barrier((own, w_in, w_out, far_outgoing))
    chunks = [own, swap_halves(own)]
    ups, downs = [chunks], [chunks]
    for step in range(1, FAR):
        pairs = [(shift_over_z(ups[-1][c], 1), shift_over_z(downs[-1][c], -1)) for c in range(2)]
        ups.append([pair[0] for pair in pairs])
        downs.append([pair[1] for pair in pairs])
        if step == 1:
            far_outgoing = lax.optimization_barrier((far_outgoing, pairs[0][0]))[0]
    far = over_experts(far_outgoing).reshape(N_EXP, 2, half_cap, LANES)

    expert_hidden = []
    for c in range(2):
        both = jnp.dot(chunks[c], w_in[0], preferred_element_type=F32)
        for step in range(1, FAR):
            if step == FAR - 1:
                both = lax.optimization_barrier(both)
            both = both + jnp.dot(ups[step][c], w_in[BLOCKS - step], preferred_element_type=F32)
            both = both + jnp.dot(downs[step][c], w_in[step], preferred_element_type=F32)
        both = both + jnp.dot(far[:, c].reshape(half_slots, LANES), w_in[FAR], preferred_element_type=F32)
        factor = lax.rsqrt(both[:, FF_LOCAL : FF_LOCAL + 1] * (1.0 / D) + 1e-05)
        gate = both[:, :FF_LANES] * factor
        up = both[:, FF_LANES:] * factor
        expert_hidden.append((gate * jax.nn.sigmoid(1.702 * gate) * (up + 1.0)).astype(BF16))

    def output_block(c, offset):
        return jnp.dot(expert_hidden[c], w_out[offset % BLOCKS], preferred_element_type=F32)

    up_sums, down_sums = [None, None], [None, None]
    for offset in range(FAR - 1, 0, -1):
        for c in range(2):
            up_sum, down_sum = output_block(c, offset), output_block(c, -offset)
            if offset < FAR - 1:
                up_sum = up_sum + up_sums[c].astype(F32)
                down_sum = down_sum + down_sums[c].astype(F32)
            up_sums[c] = shift_over_z(up_sum.astype(BF16), 1)
            down_sums[c] = shift_over_z(down_sum.astype(BF16), -1)
        if offset == FAR - 1:
            far_hidden = lax.optimization_barrier((expert_hidden[0], expert_hidden[1], up_sums[0]))[:2]
    far_value = jnp.stack(
        [
            jnp.dot(h, w_out[FAR], preferred_element_type=F32).astype(BF16).reshape(N_EXP, half_cap, LANES)
            for h in far_hidden
        ],
        axis=1,
    )
    far_mixed = shift_over_z(mixed_of(taken_both, far_value.reshape(N_EXP, CAP, LANES)), FAR)
    sums = [output_block(c, 0) + up_sums[c].astype(F32) + down_sums[c].astype(F32) for c in range(2)]
    other_sum = swap_halves(sums[0].astype(BF16))
    whole_sum = (sums[1] + other_sum.astype(F32)).astype(BF16)
    mixed = mixed_of(taken_other, whole_sum.reshape(N_EXP, half_cap, LANES)) + far_mixed

    mixed = mixed.reshape(BLOCKS, HALVES, own_rows, LANES)
    halves = jnp.arange(HALVES, dtype=jnp.int32)[None, :, None, None]
    mixed = mixed + jnp.where(halves == half, hidden_state.reshape(BLOCKS, 1, own_rows, LANES), 0.0)
    last = lax.all_to_all(mixed.reshape(N_ATTN, own_rows, LANES), "attn", 0, 0, tiled=True)
    last = jnp.sum(last.reshape(BLOCKS, HALVES, own_rows, LANES), axis=1)
    return last[:, :, :BLOCK].transpose(1, 0, 2).reshape(own_rows, D).astype(BF16)


def solution(mesh):
    in_specs = (
        P(("exp", "attn"), None),
        P(("exp", "attn"), None),
        P(("exp", "attn"), None, None, None),
        P(("exp", "attn"), None, None),
        P(),
        P("attn", None),
        P(),
        P("exp", None),
        P("exp", None),
        P("exp", None, "attn"),
        P("exp", None, "attn"),
        P("exp", "attn", None),
    )
    out_specs = P(("exp", "attn"), None)
    return jax.shard_map(local, mesh=mesh, in_specs=in_specs, out_specs=out_specs, check_vma=False)
```

```python
import jax
import jax.numpy as jnp
from jax import lax
from jax.sharding import PartitionSpec as P

HEAD_SIZE = 64
QUERY_HEADS = 32
KEY_VALUE_HEADS = 4
D = 2880
FF_LOCAL = 180
N_ATTN = 16
N_EXP = 32
CAP = 32
HALVES = 2
BLOCKS = N_ATTN // HALVES
BLOCK = D // BLOCKS
LANES = 384
FF_LANES = 256
FAR = BLOCKS // 2
F32 = jnp.float32
BF16 = jnp.bfloat16

Z_GROUPS = [[z * HALVES + half for z in range(BLOCKS)] for half in range(HALVES)]


def attend(queries, window_key_value_cache, new_key_value, head_sink_logits):
    count_of_rows = queries.shape[0]
    query_groups = QUERY_HEADS // KEY_VALUE_HEADS
    grouped_queries = queries.reshape(count_of_rows, KEY_VALUE_HEADS, query_groups, HEAD_SIZE)
    all_keys = jnp.concatenate(
        [window_key_value_cache[:, :, :, :HEAD_SIZE], new_key_value[:, :, None, :HEAD_SIZE]], axis=2
    )
    all_values = jnp.concatenate(
        [window_key_value_cache[:, :, :, HEAD_SIZE:], new_key_value[:, :, None, HEAD_SIZE:]], axis=2
    )
    scores = jnp.einsum(
        "rkgd,rkjd->rkgj", grouped_queries, all_keys, preferred_element_type=jnp.float32
    ) * HEAD_SIZE ** (-0.5)
    sink_portion = head_sink_logits.reshape(1, KEY_VALUE_HEADS, query_groups, 1)
    highest = jnp.maximum(jnp.max(scores, axis=3, keepdims=True), sink_portion)
    raised = jnp.exp(scores - highest)
    denominator = jnp.sum(raised, axis=3, keepdims=True) + jnp.exp(sink_portion - highest)
    weights = (raised / denominator).astype(jnp.bfloat16)
    combined = jnp.einsum(
        "rkgj,rkjd->rkgd", weights, all_values, preferred_element_type=jnp.float32
    )
    return combined.reshape(count_of_rows, QUERY_HEADS * HEAD_SIZE).astype(jnp.bfloat16)


def shift_over_z(array, step):
    pairs = [
        (z * HALVES + half, (z + step) % BLOCKS * HALVES + half) for z in range(BLOCKS) for half in range(HALVES)
    ]
    return lax.ppermute(array, "attn", pairs)


def swap_halves(array):
    return lax.ppermute(array, "attn", [(i, i ^ 1) for i in range(N_ATTN)])


def over_z(array):
    return lax.all_to_all(array, "attn", 0, 0, tiled=True, axis_index_groups=Z_GROUPS)


def over_experts(array):
    return lax.all_to_all(array, "exp", 0, 0, tiled=True)


def to_blocks(array):
    array = array.reshape(array.shape[:-1] + (BLOCKS, BLOCK))
    return jnp.pad(array, [(0, 0)] * (array.ndim - 1) + [(0, LANES - BLOCK)])


def local(
    residual,
    queries,
    window_key_value_cache,
    new_key_value,
    head_sink_logits,
    out_proj,
    norm_gain,
    expert_ids,
    gate_mix,
    w_gate,
    w_up,
    w_down,
):
    own_rows = residual.shape[0]
    column_rows = expert_ids.shape[0]
    half_rows = column_rows // HALVES
    half_cap = CAP // HALVES
    half_slots = N_EXP * half_cap
    attn_index = lax.axis_index("attn")
    z_index = lax.shift_right_logical(attn_index, 1)
    half = lax.bitwise_and(attn_index, 1)
    first_half = half == 0

    other_proj = swap_halves(out_proj)

    attended = attend(queries, window_key_value_cache, new_key_value, head_sink_logits)
    heads = attended.reshape(own_rows, BLOCKS, HALVES, 128)
    own_heads = jnp.where(first_half, heads[:, :, 0], heads[:, :, 1])
    other_heads = jnp.where(first_half, heads[:, :, 1], heads[:, :, 0])
    sent = jnp.concatenate([own_heads, other_heads, to_blocks(residual)], axis=2).transpose(1, 0, 2)
    got = over_z(sent).reshape(half_rows, HALVES * 128 + LANES)
    partial_sums = jnp.dot(got[:, :128], out_proj, preferred_element_type=F32)
    partial_sums = partial_sums + jnp.dot(got[:, 128:256], other_proj, preferred_element_type=F32)
    partial_sums = to_blocks(lax.optimization_barrier(partial_sums.astype(BF16))).transpose(1, 0, 2)
    hidden_state = got[:, HALVES * 128 :].astype(F32) + jnp.sum(over_z(partial_sums).astype(F32), axis=0)

    gain = lax.dynamic_index_in_dim(to_blocks(norm_gain), z_index, 0, keepdims=False)
    square = jnp.sum(hidden_state * hidden_state, axis=1, keepdims=True)
    square_high = lax.reduce_precision(square, 8, 7)
    square_low = square - square_high
    lane = lax.broadcasted_iota(jnp.int32, (half_rows, LANES), 1)
    scaled = hidden_state * gain
    scaled = jnp.where(lane == BLOCK, square_high, jnp.where(lane == BLOCK + 1, square_low, scaled)).astype(BF16)
    other_scaled = swap_halves(scaled).reshape(BLOCKS, own_rows, LANES)
    scaled = scaled.reshape(BLOCKS, own_rows, LANES)
    scaled = jnp.stack(
        [jnp.where(first_half, scaled, other_scaled), jnp.where(first_half, other_scaled, scaled)], axis=1
    ).reshape(column_rows, LANES)

    names = expert_ids.T[None, :, :] == jnp.arange(N_EXP, dtype=jnp.int32)[:, None, None]
    named = jnp.any(names, axis=1)
    weight = jnp.sum(jnp.where(names, gate_mix.T[None, :, :], 0.0), axis=1)
    row = jnp.arange(column_rows, dtype=jnp.int32)
    earlier = (row[:, None] < row[None, :]).astype(BF16)
    slot = jnp.dot(named.astype(BF16), earlier, preferred_element_type=F32).astype(jnp.int32)
    slot = jnp.where(named, slot, -1)

    def taken_of(own_half):
        base = half_cap * (half if own_half else 1 - half)
        return slot[:, None, :] == base + jnp.arange(half_cap, dtype=jnp.int32)[None, :, None]

    taken_own, taken_other = taken_of(True), taken_of(False)
    taken_both = jnp.concatenate([taken_own, taken_other], axis=1)

    def picked(taken, rows):
        select = taken.astype(BF16).reshape(-1, column_rows)
        return jnp.dot(select, rows, preferred_element_type=F32).astype(BF16).reshape(N_EXP, -1, LANES)

    def mixed_of(taken, partial_value):
        returned = over_experts(partial_value).reshape(-1, LANES)
        mix = jnp.where(taken, weight[:, None, :], 0.0).reshape(-1, column_rows)
        mix_high = lax.reduce_precision(mix, 8, 7)
        mix_low = (mix - mix_high).astype(BF16)
        over_slots = (((0,), (0,)), ((), ()))
        mixed = lax.dot_general(mix_high.astype(BF16), returned, over_slots, preferred_element_type=F32)
        return mixed + lax.dot_general(mix_low, returned, over_slots, preferred_element_type=F32)

    def padded_in(w):
        w = w.reshape(BLOCKS, BLOCK, FF_LOCAL)
        return jnp.pad(w, ((0, 0), (0, LANES - BLOCK), (0, FF_LANES - FF_LOCAL)))

    w_in = jnp.concatenate([padded_in(w_gate), padded_in(w_up)], axis=2)
    in_row = lax.broadcasted_iota(jnp.int32, w_in.shape, 1)
    in_column = lax.broadcasted_iota(jnp.int32, w_in.shape, 2)
    w_in = jnp.where((in_column == FF_LOCAL) & (in_row >= BLOCK) & (in_row < BLOCK + 2), jnp.ones((), BF16), w_in)
    w_out = jnp.pad(to_blocks(w_down[0]).transpose(1, 0, 2), ((0, 0), (0, FF_LANES - FF_LOCAL), (0, 0)))

    def at_offset(blocks, offset):
        index = lax.bitwise_and(z_index + offset % BLOCKS, BLOCKS - 1)
        return lax.dynamic_index_in_dim(blocks, index, 0, keepdims=False)

    def input_term(rows, offset):
        return jnp.dot(rows, at_offset(w_in, offset), preferred_element_type=F32)

    far_outgoing = picked(taken_both, shift_over_z(scaled, FAR))
    own = over_experts(picked(taken_own, scaled)).reshape(half_slots, LANES)
    own, w_in, w_out, far_outgoing = lax.optimization_barrier((own, w_in, w_out, far_outgoing))
    halves_of_own = [own, swap_halves(own)]
    up_block = jnp.concatenate([shift_over_z(h, 1) for h in halves_of_own])
    down_block = jnp.concatenate([shift_over_z(h, -1) for h in halves_of_own])
    both = input_term(jnp.concatenate(halves_of_own), 0) + input_term(up_block, -1)
    far_outgoing, both = lax.optimization_barrier((far_outgoing, both))
    far = over_experts(far_outgoing).reshape(N_EXP, 2, half_cap, LANES)
    both = both + input_term(down_block, 1)
    for step in range(2, FAR):
        up_block, down_block = shift_over_z(up_block, 1), shift_over_z(down_block, -1)
        if step == FAR - 1:
            both = lax.optimization_barrier(both)
        both = both + input_term(up_block, -step)
        both = both + input_term(down_block, step)
    both = both + input_term(far.transpose(1, 0, 2, 3).reshape(N_EXP * CAP, LANES), FAR)
    factor = lax.rsqrt(both[:, FF_LOCAL : FF_LOCAL + 1] * (1.0 / D) + 1e-05)
    gate = both[:, :FF_LANES] * factor
    up = both[:, FF_LANES:] * factor
    expert_hidden = (gate * jax.nn.sigmoid(1.702 * gate) * (up + 1.0)).astype(BF16)

    def output_block(offset):
        return jnp.dot(expert_hidden, at_offset(w_out, offset), preferred_element_type=F32)

    up_sum = shift_over_z(output_block(FAR - 1).astype(BF16), 1)
    down_sum = shift_over_z(output_block(1 - FAR).astype(BF16), -1)
    far_value = output_block(FAR).astype(BF16).reshape(2, N_EXP, half_cap, LANES).transpose(1, 0, 2, 3)
    far_mixed = shift_over_z(mixed_of(taken_both, far_value.reshape(N_EXP, CAP, LANES)), FAR)
    for offset in range(FAR - 2, 0, -1):
        up_sum = (output_block(offset) + up_sum.astype(F32)).astype(BF16)
        down_sum = (output_block(-offset) + down_sum.astype(F32)).astype(BF16)
        if offset > 1:
            up_sum, down_sum = shift_over_z(up_sum, 1), shift_over_z(down_sum, -1)
    own_block = output_block(0)
    sums = []
    for rows in (slice(0, half_slots), slice(half_slots, None)):
        arrived = shift_over_z(up_sum[rows], 1).astype(F32) + shift_over_z(down_sum[rows], -1).astype(F32)
        sums.append(own_block[rows] + arrived)
    other_sum = swap_halves(sums[0].astype(BF16))
    whole_sum = (sums[1] + other_sum.astype(F32)).astype(BF16)
    mixed = mixed_of(taken_other, whole_sum.reshape(N_EXP, half_cap, LANES)) + far_mixed

    mixed = mixed.reshape(BLOCKS, HALVES, own_rows, LANES)
    halves = jnp.arange(HALVES, dtype=jnp.int32)[None, :, None, None]
    mixed = mixed + jnp.where(halves == half, hidden_state.reshape(BLOCKS, 1, own_rows, LANES), 0.0)
    last = lax.all_to_all(mixed.reshape(N_ATTN, own_rows, LANES), "attn", 0, 0, tiled=True)
    last = jnp.sum(last.reshape(BLOCKS, HALVES, own_rows, LANES), axis=1)
    return last[:, :, :BLOCK].transpose(1, 0, 2).reshape(own_rows, D).astype(BF16)


def solution(mesh):
    in_specs = (
        P(("exp", "attn"), None),
        P(("exp", "attn"), None),
        P(("exp", "attn"), None, None, None),
        P(("exp", "attn"), None, None),
        P(),
        P("attn", None),
        P(),
        P("exp", None),
        P("exp", None),
        P("exp", None, "attn"),
        P("exp", None, "attn"),
        P("exp", "attn", None),
    )
    out_specs = P(("exp", "attn"), None)
    return jax.shard_map(local, mesh=mesh, in_specs=in_specs, out_specs=out_specs, check_vma=False)
```

```python
import jax
import jax.numpy as jnp
from jax import lax
from jax.experimental import pallas as pl
from jax.experimental.pallas import tpu as pltpu
from jax.sharding import PartitionSpec as P

HEAD_SIZE = 64
QUERY_HEADS = 32
KEY_VALUE_HEADS = 4
D = 2880
FF_LOCAL = 180
N_ATTN = 16
N_EXP = 32
CAP = 32
HALVES = 2
BLOCKS = N_ATTN // HALVES
BLOCK = D // BLOCKS
LANES = 384
FF_LANES = 256
Z_SLOTS = 24
Y_SLOTS = CAP - Z_SLOTS
ROW_TILE = 256
F32 = jnp.float32
BF16 = jnp.bfloat16

Z_GROUPS = [[z * HALVES + half for z in range(BLOCKS)] for half in range(HALVES)]


def attend(queries, window_key_value_cache, new_key_value, head_sink_logits):
    count_of_rows = queries.shape[0]
    query_groups = QUERY_HEADS // KEY_VALUE_HEADS
    grouped_queries = queries.reshape(count_of_rows, KEY_VALUE_HEADS, query_groups, HEAD_SIZE)
    all_keys = jnp.concatenate(
        [window_key_value_cache[:, :, :, :HEAD_SIZE], new_key_value[:, :, None, :HEAD_SIZE]], axis=2
    )
    all_values = jnp.concatenate(
        [window_key_value_cache[:, :, :, HEAD_SIZE:], new_key_value[:, :, None, HEAD_SIZE:]], axis=2
    )
    scores = jnp.einsum(
        "rkgd,rkjd->rkgj", grouped_queries, all_keys, preferred_element_type=jnp.float32
    ) * HEAD_SIZE ** (-0.5)
    sink_portion = head_sink_logits.reshape(1, KEY_VALUE_HEADS, query_groups, 1)
    highest = jnp.maximum(jnp.max(scores, axis=3, keepdims=True), sink_portion)
    raised = jnp.exp(scores - highest)
    denominator = jnp.sum(raised, axis=3, keepdims=True) + jnp.exp(sink_portion - highest)
    weights = (raised / denominator).astype(jnp.bfloat16)
    combined = jnp.einsum(
        "rkgj,rkjd->rkgd", weights, all_values, preferred_element_type=jnp.float32
    )
    return combined.reshape(count_of_rows, QUERY_HEADS * HEAD_SIZE).astype(jnp.bfloat16)


def activated(both):
    both = both * lax.rsqrt(both[:, FF_LOCAL : FF_LOCAL + 1] * (1.0 / D) + 1e-05)
    gate = both[:, :FF_LANES]
    up = both[:, FF_LANES:]
    return (gate * jax.nn.sigmoid(1.702 * gate) * (up + 1.0)).astype(BF16)


def blocks_kernel(x_ref, w_in_ref, w_out_ref, y_ref):
    both = jnp.dot(x_ref[0], w_in_ref[0], preferred_element_type=F32)
    for block in range(1, BLOCKS):
        both = both + jnp.dot(x_ref[block], w_in_ref[block], preferred_element_type=F32)
    hidden = activated(both)
    for block in range(BLOCKS):
        y_ref[block] = jnp.dot(hidden, w_out_ref[block], preferred_element_type=F32).astype(BF16)


def rows_kernel(x_ref, w_in_ref, w_out_ref, y_ref):
    both = jnp.dot(x_ref[:, :LANES], w_in_ref[0], preferred_element_type=F32)
    for block in range(1, BLOCKS):
        x = x_ref[:, block * LANES : (block + 1) * LANES]
        both = both + jnp.dot(x, w_in_ref[block], preferred_element_type=F32)
    hidden = activated(both)
    for block in range(BLOCKS):
        y = jnp.dot(hidden, w_out_ref[block], preferred_element_type=F32).astype(BF16)
        y_ref[:, block * LANES : (block + 1) * LANES] = y


def run_experts(kernel, x, w_in, w_out, rows, block_shape, index_map):
    return pl.pallas_call(
        kernel,
        grid=(rows // ROW_TILE,),
        in_specs=[
            pl.BlockSpec(block_shape, index_map),
            pl.BlockSpec(w_in.shape, lambda i: (0, 0, 0)),
            pl.BlockSpec(w_out.shape, lambda i: (0, 0, 0)),
        ],
        out_specs=pl.BlockSpec(block_shape, index_map),
        out_shape=jax.ShapeDtypeStruct(x.shape, BF16),
        compiler_params=pltpu.CompilerParams(vmem_limit_bytes=60 * 2**20),
        cost_estimate=pl.CostEstimate(
            flops=2 * rows * D * 3 * FF_LOCAL,
            bytes_accessed=4 * rows * D + 5 * 2**20,
            transcendentals=rows * FF_LOCAL,
        ),
    )(x, w_in, w_out)


def experts_on_blocks(x, w_in, w_out):
    return run_experts(blocks_kernel, x, w_in, w_out, x.shape[1], (BLOCKS, ROW_TILE, LANES), lambda i: (0, i, 0))


def experts_on_rows(x, w_in, w_out):
    return run_experts(rows_kernel, x, w_in, w_out, x.shape[0], (ROW_TILE, BLOCKS * LANES), lambda i: (i, 0))


def swap_halves(array):
    return lax.ppermute(array, "attn", [(i, i ^ 1) for i in range(N_ATTN)])


def over_z(array):
    return lax.all_to_all(array, "attn", 0, 0, tiled=True, axis_index_groups=Z_GROUPS)


def over_experts(array):
    return lax.all_to_all(array, "exp", 0, 0, tiled=True)


def to_blocks(array):
    array = array.reshape(array.shape[:-1] + (BLOCKS, BLOCK))
    return jnp.pad(array, [(0, 0)] * (array.ndim - 1) + [(0, LANES - BLOCK)])


def local(
    residual,
    queries,
    window_key_value_cache,
    new_key_value,
    head_sink_logits,
    out_proj,
    norm_gain,
    expert_ids,
    gate_mix,
    w_gate,
    w_up,
    w_down,
):
    own_rows = residual.shape[0]
    column_rows = expert_ids.shape[0]
    half_rows = column_rows // HALVES
    attn_index = lax.axis_index("attn")
    z_index = lax.shift_right_logical(attn_index, 1)
    half = lax.bitwise_and(attn_index, 1)
    first_half = half == 0

    other_proj = swap_halves(out_proj)

    attended = attend(queries, window_key_value_cache, new_key_value, head_sink_logits)
    heads = attended.reshape(own_rows, BLOCKS, HALVES, 128)
    own_heads = jnp.where(first_half, heads[:, :, 0], heads[:, :, 1])
    other_heads = jnp.where(first_half, heads[:, :, 1], heads[:, :, 0])
    sent = jnp.concatenate([own_heads, other_heads, to_blocks(residual)], axis=2).transpose(1, 0, 2)
    got = over_z(sent).reshape(half_rows, HALVES * 128 + LANES)
    partial_sums = jnp.dot(got[:, :128], out_proj, preferred_element_type=F32)
    partial_sums = partial_sums + jnp.dot(got[:, 128:256], other_proj, preferred_element_type=F32)
    partial_sums = to_blocks(lax.optimization_barrier(partial_sums.astype(BF16))).transpose(1, 0, 2)
    hidden_state = got[:, HALVES * 128 :].astype(F32) + jnp.sum(over_z(partial_sums).astype(F32), axis=0)

    gain = lax.dynamic_index_in_dim(to_blocks(norm_gain), z_index, 0, keepdims=False)
    square = jnp.sum(hidden_state * hidden_state, axis=1, keepdims=True)
    square_high = lax.reduce_precision(square, 8, 7)
    square_low = square - square_high
    lane = lax.broadcasted_iota(jnp.int32, (half_rows, LANES), 1)
    scaled = hidden_state * gain
    scaled = jnp.where(lane == BLOCK, square_high, jnp.where(lane == BLOCK + 1, square_low, scaled)).astype(BF16)
    other_scaled = swap_halves(scaled).reshape(BLOCKS, own_rows, LANES)
    scaled = scaled.reshape(BLOCKS, own_rows, LANES)
    scaled = jnp.stack(
        [jnp.where(first_half, scaled, other_scaled), jnp.where(first_half, other_scaled, scaled)], axis=1
    ).reshape(column_rows, LANES)

    names = expert_ids.T[None, :, :] == jnp.arange(N_EXP, dtype=jnp.int32)[:, None, None]
    named = jnp.any(names, axis=1)
    weight = jnp.sum(jnp.where(names, gate_mix.T[None, :, :], 0.0), axis=1)
    row = jnp.arange(column_rows, dtype=jnp.int32)
    earlier = (row[:, None] < row[None, :]).astype(BF16)
    slot = jnp.dot(named.astype(BF16), earlier, preferred_element_type=F32).astype(jnp.int32)
    slot = jnp.where(named, slot, -1)

    def taken_of(first, count):
        return slot[:, None, :] == first + jnp.arange(count, dtype=jnp.int32)[None, :, None]

    taken_z, taken_y = taken_of(0, Z_SLOTS), taken_of(Z_SLOTS, Y_SLOTS)

    def picked(taken, rows):
        select = taken.astype(BF16).reshape(-1, column_rows)
        rows = jnp.dot(select, rows, preferred_element_type=F32).astype(BF16)
        return rows.reshape(N_EXP, -1, rows.shape[1])

    def mixed_of(taken, partial_value):
        returned = over_experts(partial_value)
        returned = returned.reshape(-1, returned.shape[2])
        mix = jnp.where(taken, weight[:, None, :], 0.0).reshape(-1, column_rows)
        mix_high = lax.reduce_precision(mix, 8, 7)
        mix_low = (mix - mix_high).astype(BF16)
        over_slots = (((0,), (0,)), ((), ()))
        mixed = lax.dot_general(mix_high.astype(BF16), returned, over_slots, preferred_element_type=F32)
        return mixed + lax.dot_general(mix_low, returned, over_slots, preferred_element_type=F32)

    def padded_in(w):
        w = w.reshape(BLOCKS, BLOCK, FF_LOCAL)
        return jnp.pad(w, ((0, 0), (0, LANES - BLOCK), (0, FF_LANES - FF_LOCAL)))

    w_in = jnp.concatenate([padded_in(w_gate), padded_in(w_up)], axis=2)
    in_row = lax.broadcasted_iota(jnp.int32, w_in.shape, 1)
    in_column = lax.broadcasted_iota(jnp.int32, w_in.shape, 2)
    w_in = jnp.where((in_column == FF_LOCAL) & (in_row >= BLOCK) & (in_row < BLOCK + 2), jnp.ones((), BF16), w_in)
    w_out = jnp.pad(to_blocks(w_down[0]).transpose(1, 0, 2), ((0, 0), (0, FF_LANES - FF_LOCAL), (0, 0)))

    own = over_experts(picked(taken_z, scaled)).reshape(N_EXP * Z_SLOTS, LANES)
    whole = lax.all_gather(scaled, "attn", axis=0, axis_index_groups=Z_GROUPS)
    own, whole = lax.optimization_barrier((own, whole))
    rows_z = lax.all_gather(own, "attn", axis=0, tiled=True, axis_index_groups=Z_GROUPS)
    whole = whole.transpose(1, 0, 2).reshape(column_rows, BLOCKS * LANES)
    rows_y = over_experts(picked(taken_y, whole)).reshape(N_EXP * Y_SLOTS, BLOCKS * LANES)
    out_y = experts_on_rows(rows_y, w_in, w_out)
    rows_z, out_y = lax.optimization_barrier((rows_z, out_y))
    out_z = experts_on_blocks(rows_z.reshape(BLOCKS, N_EXP * Z_SLOTS, LANES), w_in, w_out)

    sum_z = lax.psum_scatter(
        out_z.reshape(BLOCKS * N_EXP * Z_SLOTS, LANES),
        "attn",
        scatter_dimension=0,
        tiled=True,
        axis_index_groups=Z_GROUPS,
    )
    mixed_y = mixed_of(taken_y, out_y.reshape(N_EXP, Y_SLOTS, BLOCKS * LANES)).astype(BF16)
    mixed_y = over_z(mixed_y.reshape(column_rows, BLOCKS, LANES).transpose(1, 0, 2))
    mixed_y = jnp.sum(mixed_y.astype(F32), axis=0)
    mixed = mixed_of(taken_z, sum_z.reshape(N_EXP, Z_SLOTS, LANES)) + mixed_y

    mixed = mixed.reshape(BLOCKS, HALVES, own_rows, LANES)
    halves = jnp.arange(HALVES, dtype=jnp.int32)[None, :, None, None]
    mixed = mixed + jnp.where(halves == half, hidden_state.reshape(BLOCKS, 1, own_rows, LANES), 0.0)
    last = lax.all_to_all(mixed.reshape(N_ATTN, own_rows, LANES), "attn", 0, 0, tiled=True)
    last = jnp.sum(last.reshape(BLOCKS, HALVES, own_rows, LANES), axis=1)
    return last[:, :, :BLOCK].transpose(1, 0, 2).reshape(own_rows, D).astype(BF16)


def solution(mesh):
    in_specs = (
        P(("exp", "attn"), None),
        P(("exp", "attn"), None),
        P(("exp", "attn"), None, None, None),
        P(("exp", "attn"), None, None),
        P(),
        P("attn", None),
        P(),
        P("exp", None),
        P("exp", None),
        P("exp", None, "attn"),
        P("exp", None, "attn"),
        P("exp", "attn", None),
    )
    out_specs = P(("exp", "attn"), None)
    return jax.shard_map(local, mesh=mesh, in_specs=in_specs, out_specs=out_specs, check_vma=False)
```

```python
import jax
import jax.numpy as jnp
from jax import lax
from jax.sharding import PartitionSpec as P

HEAD_SIZE = 64
QUERY_HEADS = 32
KEY_VALUE_HEADS = 4
D = 2880
FF_LOCAL = 180
N_ATTN = 16
N_EXP = 32
CAP = 32
HALVES = 2
BLOCKS = N_ATTN // HALVES
BLOCK = D // BLOCKS
LANES = 384
FF_LANES = 256
FAR = BLOCKS // 2
F32 = jnp.float32
BF16 = jnp.bfloat16

Z_GROUPS = [[z * HALVES + half for z in range(BLOCKS)] for half in range(HALVES)]


def attend(queries, window_key_value_cache, new_key_value, head_sink_logits):
    count_of_rows = queries.shape[0]
    query_groups = QUERY_HEADS // KEY_VALUE_HEADS
    grouped_queries = queries.reshape(count_of_rows, KEY_VALUE_HEADS, query_groups, HEAD_SIZE)
    all_keys = jnp.concatenate(
        [window_key_value_cache[:, :, :, :HEAD_SIZE], new_key_value[:, :, None, :HEAD_SIZE]], axis=2
    )
    all_values = jnp.concatenate(
        [window_key_value_cache[:, :, :, HEAD_SIZE:], new_key_value[:, :, None, HEAD_SIZE:]], axis=2
    )
    scores = jnp.einsum(
        "rkgd,rkjd->rkgj", grouped_queries, all_keys, preferred_element_type=jnp.float32
    ) * HEAD_SIZE ** (-0.5)
    sink_portion = head_sink_logits.reshape(1, KEY_VALUE_HEADS, query_groups, 1)
    highest = jnp.maximum(jnp.max(scores, axis=3, keepdims=True), sink_portion)
    raised = jnp.exp(scores - highest)
    denominator = jnp.sum(raised, axis=3, keepdims=True) + jnp.exp(sink_portion - highest)
    weights = (raised / denominator).astype(jnp.bfloat16)
    combined = jnp.einsum(
        "rkgj,rkjd->rkgd", weights, all_values, preferred_element_type=jnp.float32
    )
    return combined.reshape(count_of_rows, QUERY_HEADS * HEAD_SIZE).astype(jnp.bfloat16)


def shift_over_z(array, step):
    pairs = [
        (z * HALVES + half, (z + step) % BLOCKS * HALVES + half) for z in range(BLOCKS) for half in range(HALVES)
    ]
    return lax.ppermute(array, "attn", pairs)


def swap_halves(array):
    return lax.ppermute(array, "attn", [(i, i ^ 1) for i in range(N_ATTN)])


def over_z(array):
    return lax.all_to_all(array, "attn", 0, 0, tiled=True, axis_index_groups=Z_GROUPS)


def over_experts(array):
    return lax.all_to_all(array, "exp", 0, 0, tiled=True)


def to_blocks(array):
    array = array.reshape(array.shape[:-1] + (BLOCKS, BLOCK))
    return jnp.pad(array, [(0, 0)] * (array.ndim - 1) + [(0, LANES - BLOCK)])


def local(
    residual,
    queries,
    window_key_value_cache,
    new_key_value,
    head_sink_logits,
    out_proj,
    norm_gain,
    expert_ids,
    gate_mix,
    w_gate,
    w_up,
    w_down,
):
    own_rows = residual.shape[0]
    column_rows = expert_ids.shape[0]
    half_rows = column_rows // HALVES
    attn_index = lax.axis_index("attn")
    z_index = lax.shift_right_logical(attn_index, 1)
    half = lax.bitwise_and(attn_index, 1)
    first_half = half == 0

    other_proj = swap_halves(out_proj)

    attended = attend(queries, window_key_value_cache, new_key_value, head_sink_logits)
    heads = attended.reshape(own_rows, BLOCKS, HALVES, 128)
    own_heads = jnp.where(first_half, heads[:, :, 0], heads[:, :, 1])
    other_heads = jnp.where(first_half, heads[:, :, 1], heads[:, :, 0])
    sent = jnp.concatenate([own_heads, other_heads, to_blocks(residual)], axis=2).transpose(1, 0, 2)
    got = over_z(sent).reshape(half_rows, HALVES * 128 + LANES)
    partial_sums = jnp.dot(got[:, :128], out_proj, preferred_element_type=F32)
    partial_sums = partial_sums + jnp.dot(got[:, 128:256], other_proj, preferred_element_type=F32)
    partial_sums = to_blocks(lax.optimization_barrier(partial_sums.astype(BF16))).transpose(1, 0, 2)
    hidden_state = got[:, HALVES * 128 :].astype(F32) + jnp.sum(over_z(partial_sums).astype(F32), axis=0)

    gain = lax.dynamic_index_in_dim(to_blocks(norm_gain), z_index, 0, keepdims=False)
    square = jnp.sum(hidden_state * hidden_state, axis=1, keepdims=True)
    square_high = lax.reduce_precision(square, 8, 7)
    square_low = square - square_high
    lane = lax.broadcasted_iota(jnp.int32, (half_rows, LANES), 1)
    scaled = hidden_state * gain
    scaled = jnp.where(lane == BLOCK, square_high, jnp.where(lane == BLOCK + 1, square_low, scaled)).astype(BF16)
    other_scaled = swap_halves(scaled).reshape(BLOCKS, own_rows, LANES)
    scaled = scaled.reshape(BLOCKS, own_rows, LANES)
    scaled = jnp.stack(
        [jnp.where(first_half, scaled, other_scaled), jnp.where(first_half, other_scaled, scaled)], axis=1
    ).reshape(column_rows, LANES)

    names = expert_ids.T[None, :, :] == jnp.arange(N_EXP, dtype=jnp.int32)[:, None, None]
    named = jnp.any(names, axis=1)
    weight = jnp.sum(jnp.where(names, gate_mix.T[None, :, :], 0.0), axis=1)
    row = jnp.arange(column_rows, dtype=jnp.int32)
    earlier = (row[:, None] < row[None, :]).astype(BF16)
    slot = jnp.dot(named.astype(BF16), earlier, preferred_element_type=F32).astype(jnp.int32)
    slot = jnp.where(named, slot, -1)

    taken = slot[:, None, :] == jnp.arange(CAP, dtype=jnp.int32)[None, :, None]
    select = taken.astype(BF16).reshape(N_EXP * CAP, column_rows)
    mix = jnp.where(taken, weight[:, None, :], 0.0).reshape(N_EXP * CAP, column_rows)
    mix_high = lax.reduce_precision(mix, 8, 7)
    mix_low = (mix - mix_high).astype(BF16)
    mix_high = mix_high.astype(BF16)

    def picked(rows):
        return jnp.dot(select, rows, preferred_element_type=F32).astype(BF16).reshape(N_EXP, CAP, LANES)

    def mixed_of(partial_value):
        returned = over_experts(partial_value.reshape(N_EXP, CAP, LANES)).reshape(N_EXP * CAP, LANES)
        over_slots = (((0,), (0,)), ((), ()))
        mixed = lax.dot_general(mix_high, returned, over_slots, preferred_element_type=F32)
        return mixed + lax.dot_general(mix_low, returned, over_slots, preferred_element_type=F32)

    def padded_in(w):
        w = w.reshape(BLOCKS, BLOCK, FF_LOCAL)
        return jnp.pad(w, ((0, 0), (0, LANES - BLOCK), (0, FF_LANES - FF_LOCAL)))

    w_in = jnp.concatenate([padded_in(w_gate), padded_in(w_up)], axis=2)
    in_row = lax.broadcasted_iota(jnp.int32, w_in.shape, 1)
    in_column = lax.broadcasted_iota(jnp.int32, w_in.shape, 2)
    w_in = jnp.where((in_column == FF_LOCAL) & (in_row >= BLOCK) & (in_row < BLOCK + 2), jnp.ones((), BF16), w_in)
    w_out = jnp.pad(to_blocks(w_down[0]).transpose(1, 0, 2), ((0, 0), (0, FF_LANES - FF_LOCAL), (0, 0)))

    def at_offset(blocks, offset):
        index = lax.bitwise_and(z_index + offset % BLOCKS, BLOCKS - 1)
        return lax.dynamic_index_in_dim(blocks, index, 0, keepdims=False)

    def input_term(rows, offset):
        return jnp.dot(rows, at_offset(w_in, offset), preferred_element_type=F32)

    w_out = [at_offset(w_out, offset) for offset in range(BLOCKS)]

    far_outgoing = picked(shift_over_z(scaled, FAR))
    own = over_experts(picked(scaled)).reshape(N_EXP * CAP, LANES)
    own, w_in, far_outgoing, *w_out = lax.optimization_barrier((own, w_in, far_outgoing, *w_out))
    up_block, down_block = shift_over_z(own, 1), shift_over_z(own, -1)
    far = over_experts(far_outgoing).reshape(N_EXP * CAP, LANES)
    both = input_term(own, 0) + input_term(up_block, -1) + input_term(down_block, 1)
    for step in range(2, FAR):
        up_block, down_block = shift_over_z(up_block, 1), shift_over_z(down_block, -1)
        if step == FAR - 1:
            both = lax.optimization_barrier(both)
        both = both + input_term(up_block, -step)
        both = both + input_term(down_block, step)
    both = both + input_term(far, FAR)
    factor = lax.rsqrt(both[:, FF_LOCAL : FF_LOCAL + 1] * (1.0 / D) + 1e-05)
    gate = both[:, :FF_LANES] * factor
    up = both[:, FF_LANES:] * factor
    expert_hidden = (gate * jax.nn.sigmoid(1.702 * gate) * (up + 1.0)).astype(BF16)

    def output_block(offset):
        return jnp.dot(expert_hidden, w_out[offset % BLOCKS], preferred_element_type=F32)

    up_sum = shift_over_z(output_block(FAR - 1).astype(BF16), 1)
    down_sum = shift_over_z(output_block(1 - FAR).astype(BF16), -1)
    far_mixed = shift_over_z(mixed_of(output_block(FAR).astype(BF16)), FAR)
    for offset in range(FAR - 2, 0, -1):
        up_sum = shift_over_z((output_block(offset) + up_sum.astype(F32)).astype(BF16), 1)
        down_sum = shift_over_z((output_block(-offset) + down_sum.astype(F32)).astype(BF16), -1)
    own_sum = (output_block(0) + up_sum.astype(F32) + down_sum.astype(F32)).astype(BF16)
    mixed = mixed_of(own_sum) + far_mixed

    mixed = mixed.reshape(BLOCKS, HALVES, own_rows, LANES)
    halves = jnp.arange(HALVES, dtype=jnp.int32)[None, :, None, None]
    mixed = mixed + jnp.where(halves == half, hidden_state.reshape(BLOCKS, 1, own_rows, LANES), 0.0)
    last = lax.all_to_all(mixed.reshape(N_ATTN, own_rows, LANES), "attn", 0, 0, tiled=True)
    last = jnp.sum(last.reshape(BLOCKS, HALVES, own_rows, LANES), axis=1)
    return last[:, :, :BLOCK].transpose(1, 0, 2).reshape(own_rows, D).astype(BF16)


def solution(mesh):
    in_specs = (
        P(("exp", "attn"), None),
        P(("exp", "attn"), None),
        P(("exp", "attn"), None, None, None),
        P(("exp", "attn"), None, None),
        P(),
        P("attn", None),
        P(),
        P("exp", None),
        P("exp", None),
        P("exp", None, "attn"),
        P("exp", None, "attn"),
        P("exp", "attn", None),
    )
    out_specs = P(("exp", "attn"), None)
    return jax.shard_map(local, mesh=mesh, in_specs=in_specs, out_specs=out_specs, check_vma=False)
```

```python
import jax
import jax.numpy as jnp
from jax import lax
from jax.experimental import pallas as pl
from jax.experimental.pallas import tpu as pltpu
from jax.sharding import PartitionSpec as P

HEAD_SIZE = 64
QUERY_HEADS = 32
KEY_VALUE_HEADS = 4
D = 2880
FF_LOCAL = 180
N_ATTN = 16
N_EXP = 32
CAP = 32
HALVES = 2
BLOCKS = N_ATTN // HALVES
BLOCK = D // BLOCKS
LANES = 384
FF_LANES = 256
FAR = BLOCKS // 2
PAIR_TILE = 16
F32 = jnp.float32
BF16 = jnp.bfloat16

Z_GROUPS = [[z * HALVES + half for z in range(BLOCKS)] for half in range(HALVES)]


def attention_kernel(queries_ref, cache_ref, new_ref, sink_ref, out_ref):
    queries = queries_ref[...]
    cache = cache_ref[...]
    new = new_ref[...].astype(F32)
    sink = sink_ref[...]
    scale = HEAD_SIZE ** (-0.5)
    over_lanes = (((2,), (2,)), ((0,), (0,)))
    scores = lax.dot_general(queries, cache, over_lanes, preferred_element_type=F32) * scale
    new_score = jnp.sum(queries.astype(F32) * new, axis=2, keepdims=True) * scale
    top = jnp.maximum(jnp.maximum(jnp.max(scores, axis=2, keepdims=True), new_score), sink)
    raised = jnp.exp(scores - top)
    new_raised = jnp.exp(new_score - top)
    total = jnp.sum(raised, axis=2, keepdims=True) + new_raised + jnp.exp(sink - top)
    weights = (raised / total).astype(BF16)
    new_weight = (new_raised / total).astype(BF16).astype(F32)
    over_keys = (((2,), (1,)), ((0,), (0,)))
    combined = lax.dot_general(weights, cache, over_keys, preferred_element_type=F32)
    out_ref[...] = (combined + new_weight * new).astype(BF16)


def attend(queries, window_key_value_cache, new_key_value, head_sink_logits):
    rows = queries.shape[0]
    groups = QUERY_HEADS // KEY_VALUE_HEADS
    pairs = rows * KEY_VALUE_HEADS
    window, lanes = window_key_value_cache.shape[2:]
    queries = queries.reshape(pairs, groups, HEAD_SIZE)
    queries = jnp.pad(queries, ((0, 0), (0, 0), (0, lanes - HEAD_SIZE)))
    sink = head_sink_logits.reshape(1, KEY_VALUE_HEADS, groups, 1)
    sink = jnp.broadcast_to(sink, (rows, KEY_VALUE_HEADS, groups, 1)).reshape(pairs, groups, 1)

    def block(*shape):
        return pl.BlockSpec((PAIR_TILE, *shape), lambda i: (i, 0, 0))

    combined = pl.pallas_call(
        attention_kernel,
        grid=(pairs // PAIR_TILE,),
        in_specs=[block(groups, lanes), block(window, lanes), block(1, lanes), block(groups, 1)],
        out_specs=block(groups, lanes),
        out_shape=jax.ShapeDtypeStruct((pairs, groups, lanes), BF16),
        compiler_params=pltpu.CompilerParams(vmem_limit_bytes=32 * 2**20),
        cost_estimate=pl.CostEstimate(
            flops=4 * pairs * groups * window * lanes,
            bytes_accessed=2 * pairs * window * lanes,
            transcendentals=pairs * groups * window,
        ),
    )(
        queries,
        window_key_value_cache.reshape(pairs, window, lanes),
        new_key_value.reshape(pairs, 1, lanes),
        sink,
    )
    return combined[:, :, HEAD_SIZE:].reshape(rows, QUERY_HEADS * HEAD_SIZE)


def shift_over_z(array, step):
    pairs = [
        (z * HALVES + half, (z + step) % BLOCKS * HALVES + half) for z in range(BLOCKS) for half in range(HALVES)
    ]
    return lax.ppermute(array, "attn", pairs)


def swap_halves(array):
    return lax.ppermute(array, "attn", [(i, i ^ 1) for i in range(N_ATTN)])


def over_z(array):
    return lax.all_to_all(array, "attn", 0, 0, tiled=True, axis_index_groups=Z_GROUPS)


def over_experts(array):
    return lax.all_to_all(array, "exp", 0, 0, tiled=True)


def to_blocks(array):
    array = array.reshape(array.shape[:-1] + (BLOCKS, BLOCK))
    return jnp.pad(array, [(0, 0)] * (array.ndim - 1) + [(0, LANES - BLOCK)])


def local(
    residual,
    queries,
    window_key_value_cache,
    new_key_value,
    head_sink_logits,
    out_proj,
    norm_gain,
    expert_ids,
    gate_mix,
    w_gate,
    w_up,
    w_down,
):
    own_rows = residual.shape[0]
    column_rows = expert_ids.shape[0]
    half_rows = column_rows // HALVES
    attn_index = lax.axis_index("attn")
    z_index = lax.shift_right_logical(attn_index, 1)
    half = lax.bitwise_and(attn_index, 1)
    first_half = half == 0

    other_proj = swap_halves(out_proj)

    attended = attend(queries, window_key_value_cache, new_key_value, head_sink_logits)
    heads = attended.reshape(own_rows, BLOCKS, HALVES, 128)
    own_heads = jnp.where(first_half, heads[:, :, 0], heads[:, :, 1])
    other_heads = jnp.where(first_half, heads[:, :, 1], heads[:, :, 0])
    sent = jnp.concatenate([own_heads, other_heads, to_blocks(residual)], axis=2).transpose(1, 0, 2)
    got = over_z(sent).reshape(half_rows, HALVES * 128 + LANES)
    partial_sums = jnp.dot(got[:, :128], out_proj, preferred_element_type=F32)
    partial_sums = partial_sums + jnp.dot(got[:, 128:256], other_proj, preferred_element_type=F32)
    partial_sums = to_blocks(lax.optimization_barrier(partial_sums.astype(BF16))).transpose(1, 0, 2)
    hidden_state = got[:, HALVES * 128 :].astype(F32) + jnp.sum(over_z(partial_sums).astype(F32), axis=0)

    gain = lax.dynamic_index_in_dim(to_blocks(norm_gain), z_index, 0, keepdims=False)
    square = jnp.sum(hidden_state * hidden_state, axis=1, keepdims=True)
    square_high = lax.reduce_precision(square, 8, 7)
    square_low = square - square_high
    lane = lax.broadcasted_iota(jnp.int32, (half_rows, LANES), 1)
    scaled = hidden_state * gain
    scaled = jnp.where(lane == BLOCK, square_high, jnp.where(lane == BLOCK + 1, square_low, scaled)).astype(BF16)
    other_scaled = swap_halves(scaled).reshape(BLOCKS, own_rows, LANES)
    scaled = scaled.reshape(BLOCKS, own_rows, LANES)
    scaled = jnp.stack(
        [jnp.where(first_half, scaled, other_scaled), jnp.where(first_half, other_scaled, scaled)], axis=1
    ).reshape(column_rows, LANES)

    names = expert_ids.T[None, :, :] == jnp.arange(N_EXP, dtype=jnp.int32)[:, None, None]
    named = jnp.any(names, axis=1)
    weight = jnp.sum(jnp.where(names, gate_mix.T[None, :, :], 0.0), axis=1)
    row = jnp.arange(column_rows, dtype=jnp.int32)
    earlier = (row[:, None] < row[None, :]).astype(BF16)
    slot = jnp.dot(named.astype(BF16), earlier, preferred_element_type=F32).astype(jnp.int32)
    slot = jnp.where(named, slot, -1)

    taken = slot[:, None, :] == jnp.arange(CAP, dtype=jnp.int32)[None, :, None]
    select = taken.astype(BF16).reshape(N_EXP * CAP, column_rows)
    mix = jnp.where(taken, weight[:, None, :], 0.0).reshape(N_EXP * CAP, column_rows)
    mix_high = lax.reduce_precision(mix, 8, 7)
    mix_low = (mix - mix_high).astype(BF16)
    mix_high = mix_high.astype(BF16)

    def picked(rows):
        return jnp.dot(select, rows, preferred_element_type=F32).astype(BF16).reshape(N_EXP, CAP, LANES)

    def mixed_of(partial_value):
        returned = over_experts(partial_value.reshape(N_EXP, CAP, LANES)).reshape(N_EXP * CAP, LANES)
        over_slots = (((0,), (0,)), ((), ()))
        mixed = lax.dot_general(mix_high, returned, over_slots, preferred_element_type=F32)
        return mixed + lax.dot_general(mix_low, returned, over_slots, preferred_element_type=F32)

    def padded_in(w):
        w = w.reshape(BLOCKS, BLOCK, FF_LOCAL)
        return jnp.pad(w, ((0, 0), (0, LANES - BLOCK), (0, FF_LANES - FF_LOCAL)))

    scaled, w_gate, w_up, w_down = lax.optimization_barrier((scaled, w_gate, w_up, w_down))
    w_in = jnp.concatenate([padded_in(w_gate), padded_in(w_up)], axis=2)
    in_row = lax.broadcasted_iota(jnp.int32, w_in.shape, 1)
    in_column = lax.broadcasted_iota(jnp.int32, w_in.shape, 2)
    w_in = jnp.where((in_column == FF_LOCAL) & (in_row >= BLOCK) & (in_row < BLOCK + 2), jnp.ones((), BF16), w_in)
    w_out = jnp.pad(to_blocks(w_down[0]).transpose(1, 0, 2), ((0, 0), (0, FF_LANES - FF_LOCAL), (0, 0)))

    def at_offset(blocks, offset):
        index = lax.bitwise_and(z_index + offset % BLOCKS, BLOCKS - 1)
        return lax.dynamic_index_in_dim(blocks, index, 0, keepdims=False)

    def input_term(rows, offset):
        return jnp.dot(rows, at_offset(w_in, offset), preferred_element_type=F32)

    w_out = [at_offset(w_out, offset) for offset in range(BLOCKS)]

    far_outgoing = picked(shift_over_z(scaled, FAR))
    own = over_experts(picked(scaled)).reshape(N_EXP * CAP, LANES)
    own, w_in, far_outgoing, *w_out = lax.optimization_barrier((own, w_in, far_outgoing, *w_out))
    up_block, down_block = shift_over_z(own, 1), shift_over_z(own, -1)
    far = over_experts(far_outgoing).reshape(N_EXP * CAP, LANES)
    both = input_term(own, 0) + input_term(up_block, -1) + input_term(down_block, 1)
    for step in range(2, FAR):
        up_block, down_block = shift_over_z(up_block, 1), shift_over_z(down_block, -1)
        if step == FAR - 1:
            both = lax.optimization_barrier(both)
        both = both + input_term(up_block, -step)
        both = both + input_term(down_block, step)
    both = both + input_term(far, FAR)
    factor = lax.rsqrt(both[:, FF_LOCAL : FF_LOCAL + 1] * (1.0 / D) + 1e-05)
    gate = both[:, :FF_LANES] * factor
    up = both[:, FF_LANES:] * factor
    expert_hidden = (gate * jax.nn.sigmoid(1.702 * gate) * (up + 1.0)).astype(BF16)

    def output_block(offset):
        return jnp.dot(expert_hidden, w_out[offset % BLOCKS], preferred_element_type=F32)

    up_sum = shift_over_z(output_block(FAR - 1).astype(BF16), 1)
    down_sum = shift_over_z(output_block(1 - FAR).astype(BF16), -1)
    far_mixed = shift_over_z(mixed_of(output_block(FAR).astype(BF16)), FAR)
    for offset in range(FAR - 2, 0, -1):
        up_sum = shift_over_z((output_block(offset) + up_sum.astype(F32)).astype(BF16), 1)
        down_sum = shift_over_z((output_block(-offset) + down_sum.astype(F32)).astype(BF16), -1)
    own_sum = (output_block(0) + up_sum.astype(F32) + down_sum.astype(F32)).astype(BF16)
    mixed = mixed_of(own_sum) + far_mixed

    mixed = mixed.reshape(BLOCKS, HALVES, own_rows, LANES)
    halves = jnp.arange(HALVES, dtype=jnp.int32)[None, :, None, None]
    mixed = mixed + jnp.where(halves == half, hidden_state.reshape(BLOCKS, 1, own_rows, LANES), 0.0)
    last = lax.all_to_all(mixed.reshape(N_ATTN, own_rows, LANES), "attn", 0, 0, tiled=True)
    last = jnp.sum(last.reshape(BLOCKS, HALVES, own_rows, LANES), axis=1)
    return last[:, :, :BLOCK].transpose(1, 0, 2).reshape(own_rows, D).astype(BF16)


def solution(mesh):
    in_specs = (
        P(("exp", "attn"), None),
        P(("exp", "attn"), None),
        P(("exp", "attn"), None, None, None),
        P(("exp", "attn"), None, None),
        P(),
        P("attn", None),
        P(),
        P("exp", None),
        P("exp", None),
        P("exp", None, "attn"),
        P("exp", None, "attn"),
        P("exp", "attn", None),
    )
    out_specs = P(("exp", "attn"), None)
    return jax.shard_map(local, mesh=mesh, in_specs=in_specs, out_specs=out_specs, check_vma=False)
```

```python
import jax
import jax.numpy as jnp
from jax import lax
from jax.experimental import pallas as pl
from jax.experimental.pallas import tpu as pltpu
from jax.sharding import PartitionSpec as P

HEAD_SIZE = 64
QUERY_HEADS = 32
KEY_VALUE_HEADS = 4
D = 2880
FF_LOCAL = 180
N_ATTN = 16
N_EXP = 32
CAP = 32
HALVES = 2
BLOCKS = N_ATTN // HALVES
BLOCK = D // BLOCKS
LANES = 384
FF_LANES = 256
FAR = BLOCKS // 2
PAIR_TILE = 16
F32 = jnp.float32
BF16 = jnp.bfloat16

Z_GROUPS = [[z * HALVES + half for z in range(BLOCKS)] for half in range(HALVES)]


def attention_kernel(queries_ref, cache_ref, new_ref, sink_ref, out_ref):
    queries = queries_ref[...]
    cache = cache_ref[...]
    new = new_ref[...].astype(F32)
    sink = sink_ref[...]
    scale = HEAD_SIZE ** (-0.5)
    over_lanes = (((2,), (2,)), ((0,), (0,)))
    scores = lax.dot_general(queries, cache, over_lanes, preferred_element_type=F32) * scale
    new_score = jnp.sum(queries.astype(F32) * new, axis=2, keepdims=True) * scale
    top = jnp.maximum(jnp.maximum(jnp.max(scores, axis=2, keepdims=True), new_score), sink)
    raised = jnp.exp(scores - top)
    new_raised = jnp.exp(new_score - top)
    total = jnp.sum(raised, axis=2, keepdims=True) + new_raised + jnp.exp(sink - top)
    weights = (raised / total).astype(BF16)
    new_weight = (new_raised / total).astype(BF16).astype(F32)
    over_keys = (((2,), (1,)), ((0,), (0,)))
    combined = lax.dot_general(weights, cache, over_keys, preferred_element_type=F32)
    out_ref[...] = (combined + new_weight * new).astype(BF16)


def attend(queries, window_key_value_cache, new_key_value, head_sink_logits):
    rows = queries.shape[0]
    groups = QUERY_HEADS // KEY_VALUE_HEADS
    pairs = rows * KEY_VALUE_HEADS
    window, lanes = window_key_value_cache.shape[2:]
    queries = queries.reshape(pairs, groups, HEAD_SIZE)
    queries = jnp.pad(queries, ((0, 0), (0, 0), (0, lanes - HEAD_SIZE)))
    sink = head_sink_logits.reshape(1, KEY_VALUE_HEADS, groups, 1)
    sink = jnp.broadcast_to(sink, (rows, KEY_VALUE_HEADS, groups, 1)).reshape(pairs, groups, 1)

    def block(*shape):
        return pl.BlockSpec((PAIR_TILE, *shape), lambda i: (i, 0, 0))

    combined = pl.pallas_call(
        attention_kernel,
        grid=(pairs // PAIR_TILE,),
        in_specs=[block(groups, lanes), block(window, lanes), block(1, lanes), block(groups, 1)],
        out_specs=block(groups, lanes),
        out_shape=jax.ShapeDtypeStruct((pairs, groups, lanes), BF16),
        compiler_params=pltpu.CompilerParams(vmem_limit_bytes=32 * 2**20),
        cost_estimate=pl.CostEstimate(
            flops=4 * pairs * groups * window * lanes,
            bytes_accessed=2 * pairs * window * lanes,
            transcendentals=pairs * groups * window,
        ),
    )(
        queries,
        window_key_value_cache.reshape(pairs, window, lanes),
        new_key_value.reshape(pairs, 1, lanes),
        sink,
    )
    return combined[:, :, HEAD_SIZE:].reshape(rows, QUERY_HEADS * HEAD_SIZE)


def shift_over_z(array, step):
    pairs = [
        (z * HALVES + half, (z + step) % BLOCKS * HALVES + half) for z in range(BLOCKS) for half in range(HALVES)
    ]
    return lax.ppermute(array, "attn", pairs)


def swap_halves(array):
    return lax.ppermute(array, "attn", [(i, i ^ 1) for i in range(N_ATTN)])


def over_z(array):
    return lax.all_to_all(array, "attn", 0, 0, tiled=True, axis_index_groups=Z_GROUPS)


def over_experts(array):
    return lax.all_to_all(array, "exp", 0, 0, tiled=True)


def to_blocks(array):
    array = array.reshape(array.shape[:-1] + (BLOCKS, BLOCK))
    return jnp.pad(array, [(0, 0)] * (array.ndim - 1) + [(0, LANES - BLOCK)])


def local(
    residual,
    queries,
    window_key_value_cache,
    new_key_value,
    head_sink_logits,
    out_proj,
    norm_gain,
    expert_ids,
    gate_mix,
    w_gate,
    w_up,
    w_down,
):
    own_rows = residual.shape[0]
    column_rows = expert_ids.shape[0]
    half_rows = column_rows // HALVES
    attn_index = lax.axis_index("attn")
    z_index = lax.shift_right_logical(attn_index, 1)
    half = lax.bitwise_and(attn_index, 1)
    first_half = half == 0

    other_proj = swap_halves(out_proj)

    attended = attend(queries, window_key_value_cache, new_key_value, head_sink_logits)
    heads = attended.reshape(own_rows, BLOCKS, HALVES, 128)
    own_heads = jnp.where(first_half, heads[:, :, 0], heads[:, :, 1])
    other_heads = jnp.where(first_half, heads[:, :, 1], heads[:, :, 0])
    sent = jnp.concatenate([own_heads, other_heads, to_blocks(residual)], axis=2).transpose(1, 0, 2)
    got = over_z(sent).reshape(half_rows, HALVES * 128 + LANES)
    partial_sums = jnp.dot(got[:, :128], out_proj, preferred_element_type=F32)
    partial_sums = partial_sums + jnp.dot(got[:, 128:256], other_proj, preferred_element_type=F32)
    partial_sums = to_blocks(lax.optimization_barrier(partial_sums.astype(BF16))).transpose(1, 0, 2)
    hidden_state = got[:, HALVES * 128 :].astype(F32) + jnp.sum(over_z(partial_sums).astype(F32), axis=0)

    gain = lax.dynamic_index_in_dim(to_blocks(norm_gain), z_index, 0, keepdims=False)
    square = jnp.sum(hidden_state * hidden_state, axis=1, keepdims=True)
    square_high = lax.reduce_precision(square, 8, 7)
    square_low = square - square_high
    lane = lax.broadcasted_iota(jnp.int32, (half_rows, LANES), 1)
    scaled = hidden_state * gain
    scaled = jnp.where(lane == BLOCK, square_high, jnp.where(lane == BLOCK + 1, square_low, scaled)).astype(BF16)
    other_scaled = swap_halves(scaled).reshape(BLOCKS, own_rows, LANES)
    scaled = scaled.reshape(BLOCKS, own_rows, LANES)
    scaled = jnp.stack(
        [jnp.where(first_half, scaled, other_scaled), jnp.where(first_half, other_scaled, scaled)], axis=1
    ).reshape(column_rows, LANES)

    names = expert_ids.T[None, :, :] == jnp.arange(N_EXP, dtype=jnp.int32)[:, None, None]
    named = jnp.any(names, axis=1)
    weight = jnp.sum(jnp.where(names, gate_mix.T[None, :, :], 0.0), axis=1)
    row = jnp.arange(column_rows, dtype=jnp.int32)
    earlier = (row[:, None] < row[None, :]).astype(BF16)
    slot = jnp.dot(named.astype(BF16), earlier, preferred_element_type=F32).astype(jnp.int32)
    slot = jnp.where(named, slot, -1)

    taken = slot[:, None, :] == jnp.arange(CAP, dtype=jnp.int32)[None, :, None]
    select = taken.astype(BF16).reshape(N_EXP * CAP, column_rows)
    mix = jnp.where(taken, weight[:, None, :], 0.0).reshape(N_EXP * CAP, column_rows)
    mix_high = lax.reduce_precision(mix, 8, 7)
    mix_low = (mix - mix_high).astype(BF16)
    mix_high = mix_high.astype(BF16)

    def picked(rows):
        return jnp.dot(select, rows, preferred_element_type=F32).astype(BF16).reshape(N_EXP, CAP, LANES)

    def mixed_of(partial_value):
        returned = over_experts(partial_value.reshape(N_EXP, CAP, LANES)).reshape(N_EXP * CAP, LANES)
        over_slots = (((0,), (0,)), ((), ()))
        mixed = lax.dot_general(mix_high, returned, over_slots, preferred_element_type=F32)
        return mixed + lax.dot_general(mix_low, returned, over_slots, preferred_element_type=F32)

    def padded_in(w):
        w = w.reshape(BLOCKS, BLOCK, FF_LOCAL)
        return jnp.pad(w, ((0, 0), (0, LANES - BLOCK), (0, FF_LANES - FF_LOCAL)))

    def at_offset(blocks, offset):
        index = lax.bitwise_and(z_index + offset % BLOCKS, BLOCKS - 1)
        return lax.dynamic_index_in_dim(blocks, index, 0, keepdims=False)

    def input_term(rows, offset):
        return jnp.dot(rows, at_offset(w_in, offset), preferred_element_type=F32)

    far_outgoing = picked(shift_over_z(scaled, FAR))
    own = over_experts(picked(scaled)).reshape(N_EXP * CAP, LANES)
    own, far_outgoing, w_gate, w_up = lax.optimization_barrier((own, far_outgoing, w_gate, w_up))
    w_in = jnp.concatenate([padded_in(w_gate), padded_in(w_up)], axis=2)
    in_row = lax.broadcasted_iota(jnp.int32, w_in.shape, 1)
    in_column = lax.broadcasted_iota(jnp.int32, w_in.shape, 2)
    w_in = jnp.where((in_column == FF_LOCAL) & (in_row >= BLOCK) & (in_row < BLOCK + 2), jnp.ones((), BF16), w_in)
    up_block, down_block = shift_over_z(own, 1), shift_over_z(own, -1)
    up_block, w_down = lax.optimization_barrier((up_block, w_down))
    w_out = jnp.pad(to_blocks(w_down[0]).transpose(1, 0, 2), ((0, 0), (0, FF_LANES - FF_LOCAL), (0, 0)))
    far = over_experts(far_outgoing).reshape(N_EXP * CAP, LANES)
    both = input_term(own, 0) + input_term(up_block, -1) + input_term(down_block, 1)
    for step in range(2, FAR):
        up_block, down_block = shift_over_z(up_block, 1), shift_over_z(down_block, -1)
        if step == FAR - 1:
            both = lax.optimization_barrier(both)
        both = both + input_term(up_block, -step)
        both = both + input_term(down_block, step)
    both = both + input_term(far, FAR)
    factor = lax.rsqrt(both[:, FF_LOCAL : FF_LOCAL + 1] * (1.0 / D) + 1e-05)
    gate = both[:, :FF_LANES] * factor
    up = both[:, FF_LANES:] * factor
    expert_hidden = (gate * jax.nn.sigmoid(1.702 * gate) * (up + 1.0)).astype(BF16)

    def output_block(offset):
        return jnp.dot(expert_hidden, at_offset(w_out, offset), preferred_element_type=F32)

    up_sum = shift_over_z(output_block(FAR - 1).astype(BF16), 1)
    down_sum = shift_over_z(output_block(1 - FAR).astype(BF16), -1)
    far_mixed = shift_over_z(mixed_of(output_block(FAR).astype(BF16)), FAR)
    for offset in range(FAR - 2, 0, -1):
        up_sum = shift_over_z((output_block(offset) + up_sum.astype(F32)).astype(BF16), 1)
        down_sum = shift_over_z((output_block(-offset) + down_sum.astype(F32)).astype(BF16), -1)
    own_sum = (output_block(0) + up_sum.astype(F32) + down_sum.astype(F32)).astype(BF16)
    mixed = mixed_of(own_sum) + far_mixed

    mixed = mixed.reshape(BLOCKS, HALVES, own_rows, LANES)
    halves = jnp.arange(HALVES, dtype=jnp.int32)[None, :, None, None]
    mixed = mixed + jnp.where(halves == half, hidden_state.reshape(BLOCKS, 1, own_rows, LANES), 0.0)
    last = lax.all_to_all(mixed.reshape(N_ATTN, own_rows, LANES), "attn", 0, 0, tiled=True)
    last = jnp.sum(last.reshape(BLOCKS, HALVES, own_rows, LANES), axis=1)
    return last[:, :, :BLOCK].transpose(1, 0, 2).reshape(own_rows, D).astype(BF16)


def solution(mesh):
    in_specs = (
        P(("exp", "attn"), None),
        P(("exp", "attn"), None),
        P(("exp", "attn"), None, None, None),
        P(("exp", "attn"), None, None),
        P(),
        P("attn", None),
        P(),
        P("exp", None),
        P("exp", None),
        P("exp", None, "attn"),
        P("exp", None, "attn"),
        P("exp", "attn", None),
    )
    out_specs = P(("exp", "attn"), None)
    return jax.shard_map(local, mesh=mesh, in_specs=in_specs, out_specs=out_specs, check_vma=False)
```

```python
import jax
import jax.numpy as jnp
from jax import lax
from jax.experimental import pallas as pl
from jax.experimental.pallas import tpu as pltpu
from jax.sharding import PartitionSpec as P

HEAD_SIZE = 64
QUERY_HEADS = 32
KEY_VALUE_HEADS = 4
D = 2880
FF_LOCAL = 180
N_ATTN = 16
N_EXP = 32
CAP = 32
HALVES = 2
BLOCKS = N_ATTN // HALVES
BLOCK = D // BLOCKS
LANES = 384
FF_LANES = 256
FAR = BLOCKS // 2
PAIR_TILE = 16
F32 = jnp.float32
BF16 = jnp.bfloat16

Z_GROUPS = [[z * HALVES + half for z in range(BLOCKS)] for half in range(HALVES)]


def attention_kernel(queries_ref, cache_ref, new_ref, sink_ref, out_ref):
    queries = queries_ref[...]
    cache = cache_ref[...]
    new = new_ref[...].astype(F32)
    sink = sink_ref[...]
    scale = HEAD_SIZE ** (-0.5)
    over_lanes = (((2,), (2,)), ((0,), (0,)))
    scores = lax.dot_general(queries, cache, over_lanes, preferred_element_type=F32) * scale
    new_score = jnp.sum(queries.astype(F32) * new, axis=2, keepdims=True) * scale
    top = jnp.maximum(jnp.maximum(jnp.max(scores, axis=2, keepdims=True), new_score), sink)
    raised = jnp.exp(scores - top)
    new_raised = jnp.exp(new_score - top)
    total = jnp.sum(raised, axis=2, keepdims=True) + new_raised + jnp.exp(sink - top)
    weights = (raised / total).astype(BF16)
    new_weight = (new_raised / total).astype(BF16).astype(F32)
    over_keys = (((2,), (1,)), ((0,), (0,)))
    combined = lax.dot_general(weights, cache, over_keys, preferred_element_type=F32)
    out_ref[...] = (combined + new_weight * new).astype(BF16)


def attend(queries, window_key_value_cache, new_key_value, head_sink_logits):
    rows = queries.shape[0]
    groups = QUERY_HEADS // KEY_VALUE_HEADS
    pairs = rows * KEY_VALUE_HEADS
    window, lanes = window_key_value_cache.shape[2:]
    queries = queries.reshape(pairs, groups, HEAD_SIZE)
    queries = jnp.pad(queries, ((0, 0), (0, 0), (0, lanes - HEAD_SIZE)))
    sink = head_sink_logits.reshape(1, KEY_VALUE_HEADS, groups, 1)
    sink = jnp.broadcast_to(sink, (rows, KEY_VALUE_HEADS, groups, 1)).reshape(pairs, groups, 1)

    def block(*shape):
        return pl.BlockSpec((PAIR_TILE, *shape), lambda i: (i, 0, 0))

    combined = pl.pallas_call(
        attention_kernel,
        grid=(pairs // PAIR_TILE,),
        in_specs=[block(groups, lanes), block(window, lanes), block(1, lanes), block(groups, 1)],
        out_specs=block(groups, lanes),
        out_shape=jax.ShapeDtypeStruct((pairs, groups, lanes), BF16),
        compiler_params=pltpu.CompilerParams(vmem_limit_bytes=32 * 2**20),
        cost_estimate=pl.CostEstimate(
            flops=4 * pairs * groups * window * lanes,
            bytes_accessed=2 * pairs * window * lanes,
            transcendentals=pairs * groups * window,
        ),
    )(
        queries,
        window_key_value_cache.reshape(pairs, window, lanes),
        new_key_value.reshape(pairs, 1, lanes),
        sink,
    )
    return combined[:, :, HEAD_SIZE:].reshape(rows, QUERY_HEADS * HEAD_SIZE)


def shift_over_z(array, step):
    pairs = [
        (z * HALVES + half, (z + step) % BLOCKS * HALVES + half) for z in range(BLOCKS) for half in range(HALVES)
    ]
    return lax.ppermute(array, "attn", pairs)


def swap_halves(array):
    return lax.ppermute(array, "attn", [(i, i ^ 1) for i in range(N_ATTN)])


def over_z(array):
    return lax.all_to_all(array, "attn", 0, 0, tiled=True, axis_index_groups=Z_GROUPS)


def over_experts(array):
    return lax.all_to_all(array, "exp", 0, 0, tiled=True)


def to_blocks(array):
    array = array.reshape(array.shape[:-1] + (BLOCKS, BLOCK))
    return jnp.pad(array, [(0, 0)] * (array.ndim - 1) + [(0, LANES - BLOCK)])


def local(
    residual,
    queries,
    window_key_value_cache,
    new_key_value,
    head_sink_logits,
    out_proj,
    norm_gain,
    expert_ids,
    gate_mix,
    w_gate,
    w_up,
    w_down,
):
    own_rows = residual.shape[0]
    column_rows = expert_ids.shape[0]
    half_rows = column_rows // HALVES
    attn_index = lax.axis_index("attn")
    z_index = lax.shift_right_logical(attn_index, 1)
    half = lax.bitwise_and(attn_index, 1)
    first_half = half == 0

    other_proj = swap_halves(out_proj)

    attended = attend(queries, window_key_value_cache, new_key_value, head_sink_logits)
    heads = attended.reshape(own_rows, BLOCKS, HALVES, 128)
    own_heads = jnp.where(first_half, heads[:, :, 0], heads[:, :, 1])
    other_heads = jnp.where(first_half, heads[:, :, 1], heads[:, :, 0])
    sent = jnp.concatenate([own_heads, other_heads, to_blocks(residual)], axis=2).transpose(1, 0, 2)
    got = over_z(sent).reshape(half_rows, HALVES * 128 + LANES)
    partial_sums = jnp.dot(got[:, :128], out_proj, preferred_element_type=F32)
    partial_sums = partial_sums + jnp.dot(got[:, 128:256], other_proj, preferred_element_type=F32)
    partial_sums = to_blocks(lax.optimization_barrier(partial_sums.astype(BF16))).transpose(1, 0, 2)
    hidden_state = got[:, HALVES * 128 :].astype(F32) + jnp.sum(over_z(partial_sums).astype(F32), axis=0)

    gain = lax.dynamic_index_in_dim(to_blocks(norm_gain), z_index, 0, keepdims=False)
    square = jnp.sum(hidden_state * hidden_state, axis=1, keepdims=True)
    square_high = lax.reduce_precision(square, 8, 7)
    square_low = square - square_high
    lane = lax.broadcasted_iota(jnp.int32, (half_rows, LANES), 1)
    scaled = hidden_state * gain
    scaled = jnp.where(lane == BLOCK, square_high, jnp.where(lane == BLOCK + 1, square_low, scaled)).astype(BF16)
    other_scaled = swap_halves(scaled).reshape(BLOCKS, own_rows, LANES)
    scaled = scaled.reshape(BLOCKS, own_rows, LANES)
    scaled = jnp.stack(
        [jnp.where(first_half, scaled, other_scaled), jnp.where(first_half, other_scaled, scaled)], axis=1
    ).reshape(column_rows, LANES)

    names = expert_ids.T[None, :, :] == jnp.arange(N_EXP, dtype=jnp.int32)[:, None, None]
    named = jnp.any(names, axis=1)
    weight = jnp.sum(jnp.where(names, gate_mix.T[None, :, :], 0.0), axis=1)
    row = jnp.arange(column_rows, dtype=jnp.int32)
    earlier = (row[:, None] < row[None, :]).astype(BF16)
    slot = jnp.dot(named.astype(BF16), earlier, preferred_element_type=F32).astype(jnp.int32)
    slot = jnp.where(named, slot, -1)

    taken = slot[:, None, :] == jnp.arange(CAP, dtype=jnp.int32)[None, :, None]
    select = taken.astype(BF16).reshape(N_EXP * CAP, column_rows)
    mix = jnp.where(taken, weight[:, None, :], 0.0).reshape(N_EXP * CAP, column_rows)
    mix_high = lax.reduce_precision(mix, 8, 7)
    mix_low = (mix - mix_high).astype(BF16)
    mix_high = mix_high.astype(BF16)

    def picked(rows):
        return jnp.dot(select, rows, preferred_element_type=F32).astype(BF16).reshape(N_EXP, CAP, LANES)

    def mixed_of(partial_value):
        returned = over_experts(partial_value.reshape(N_EXP, CAP, LANES)).reshape(N_EXP * CAP, LANES)
        over_slots = (((0,), (0,)), ((), ()))
        mixed = lax.dot_general(mix_high, returned, over_slots, preferred_element_type=F32)
        return mixed + lax.dot_general(mix_low, returned, over_slots, preferred_element_type=F32)

    def padded_in(w):
        w = w.reshape(BLOCKS, BLOCK, FF_LOCAL)
        return jnp.pad(w, ((0, 0), (0, LANES - BLOCK), (0, FF_LANES - FF_LOCAL)))

    def at_offset(blocks, offset):
        index = lax.bitwise_and(z_index + offset % BLOCKS, BLOCKS - 1)
        return lax.dynamic_index_in_dim(blocks, index, 0, keepdims=False)

    def input_term(rows, offset):
        return jnp.dot(rows, at_offset(w_in, offset), preferred_element_type=F32)

    far_outgoing = picked(shift_over_z(scaled, FAR))
    own = over_experts(picked(scaled)).reshape(N_EXP * CAP, LANES)
    own, far_outgoing, w_gate, w_up = lax.optimization_barrier((own, far_outgoing, w_gate, w_up))
    w_in = jnp.concatenate([padded_in(w_gate), padded_in(w_up)], axis=2)
    in_row = lax.broadcasted_iota(jnp.int32, w_in.shape, 1)
    in_column = lax.broadcasted_iota(jnp.int32, w_in.shape, 2)
    w_in = jnp.where((in_column == FF_LOCAL) & (in_row >= BLOCK) & (in_row < BLOCK + 2), jnp.ones((), BF16), w_in)
    up_block, down_block = shift_over_z(own, 1), shift_over_z(own, -1)
    up_block, w_down = lax.optimization_barrier((up_block, w_down))
    w_out = jnp.pad(to_blocks(w_down[0]).transpose(1, 0, 2), ((0, 0), (0, FF_LANES - FF_LOCAL), (0, 0)))
    far = over_experts(far_outgoing).reshape(N_EXP * CAP, LANES)
    both = input_term(own, 0) + input_term(up_block, -1) + input_term(down_block, 1)
    for step in range(2, FAR):
        up_block, down_block = shift_over_z(up_block, 1), shift_over_z(down_block, -1)
        if step == FAR - 1:
            both = lax.optimization_barrier(both)
        both = both + input_term(up_block, -step)
        both = both + input_term(down_block, step)
    both = both + input_term(far, FAR)
    factor = lax.rsqrt(both[:, FF_LOCAL : FF_LOCAL + 1] * (1.0 / D) + 1e-05)
    gate = both[:, :FF_LANES] * factor
    up = both[:, FF_LANES:] * factor
    expert_hidden = (gate * jax.nn.sigmoid(1.702 * gate) * (up + 1.0)).astype(BF16)

    def output_block(offset):
        return jnp.dot(expert_hidden, at_offset(w_out, offset), preferred_element_type=F32)

    up_sum = shift_over_z(output_block(FAR - 1).astype(BF16), 1)
    down_sum = shift_over_z(output_block(1 - FAR).astype(BF16), -1)
    far_mixed = shift_over_z(mixed_of(output_block(FAR).astype(BF16)), FAR)
    for offset in range(FAR - 2, 0, -1):
        up_sum = shift_over_z((output_block(offset) + up_sum.astype(F32)).astype(BF16), 1)
        down_sum = shift_over_z((output_block(-offset) + down_sum.astype(F32)).astype(BF16), -1)
    own_sum = (output_block(0) + up_sum.astype(F32) + down_sum.astype(F32)).astype(BF16)
    mixed = mixed_of(own_sum) + far_mixed

    mixed = mixed.reshape(BLOCKS, HALVES, own_rows, LANES)
    halves = jnp.arange(HALVES, dtype=jnp.int32)[None, :, None, None]
    mixed = mixed + jnp.where(halves == half, hidden_state.reshape(BLOCKS, 1, own_rows, LANES), 0.0)
    mixed = mixed.reshape(N_ATTN, own_rows, LANES).astype(BF16)
    last = lax.all_to_all(mixed, "attn", 0, 0, tiled=True).astype(F32)
    last = jnp.sum(last.reshape(BLOCKS, HALVES, own_rows, LANES), axis=1)
    return last[:, :, :BLOCK].transpose(1, 0, 2).reshape(own_rows, D).astype(BF16)


def solution(mesh):
    in_specs = (
        P(("exp", "attn"), None),
        P(("exp", "attn"), None),
        P(("exp", "attn"), None, None, None),
        P(("exp", "attn"), None, None),
        P(),
        P("attn", None),
        P(),
        P("exp", None),
        P("exp", None),
        P("exp", None, "attn"),
        P("exp", None, "attn"),
        P("exp", "attn", None),
    )
    out_specs = P(("exp", "attn"), None)
    return jax.shard_map(local, mesh=mesh, in_specs=in_specs, out_specs=out_specs, check_vma=False)
```
